128 devices in a mesh: weld: 8 (over x, core), trans: 16 (over z, y).
Axes of the slice: x: 4, y: 4, z: 4, core: 2. Of those that a mesh axis runs over, the one named last changes fastest.
Arguments:
- weights: bfloat16 [49152, 64, 256], P(('weld', 'trans'))
- particle_state: float32 [10, 3145728], P(None, ('weld', 'trans')), may hold values from -6 to 6
- mass: float32 [3145728], P(('weld', 'trans')), may hold values from 0.5 to 2
- stiffness: float32 [3145728], P(('weld', 'trans')), may hold values from 1 to 10
- targets: int32 [49152], P(('weld', 'trans')), may hold values from 0 to 8191, as said below
- counts: int32 [49152], P(('weld', 'trans')), may hold values from 0 to 64, as said below
- partner_bit: int32 [128], P(('weld', 'trans')), may hold values from 0 to 1, as said below
- swap_list: int32 [128, 24], P(('weld', 'trans')), may hold values from 0 to 383, as said below
Outputs:
- particle_next: float32 [10, 3145728], P(None, ('weld', 'trans'))
- node_fields: bfloat16 [8192, 256], P(('weld', 'trans'))
The draws below stay inside these ranges and needn't reach their ends.
Inputs may be any that keep to these rules, and one draw needn't show every extreme that they name: `partner_bit`: equal for all devices with the same trans index, so that partners agree. `swap_list`: each row holds 24 different local block indices. `targets`: node block g belongs to device g // 64. After the swap, at most 4 blocks of one device name node blocks of any one device, and exactly 4 name node blocks of the device itself. `counts`: every device has a full block.
All inputs are finite; a program needn't handle non-finite values.
Results may differ from the reference program's by a relative error of at most 0.005.
Values may be sent and summed in bfloat16 or wider, within the bound.
A program may use at most 192 MiB of HBM per device.

```python
import math
import jax
import jax.numpy as jnp
from jax import lax

BS = 64
PB = 384
NBD = 64
STEPS = 2
OWNERS = 128
CAP = 4
SW = 24
P_BLOCKS = 49152
PARTICLES = 3145728
NODE_BLOCKS = 8192
N_WELD = 8
N_TRANS = 16


def pairing(key):
    bits_row = jax.random.randint(jax.random.fold_in(key, 101), (N_TRANS,), 0, 2).astype(jnp.int32)
    bits_all = jnp.tile(bits_row, N_WELD)
    list_keys = jax.random.split(jax.random.fold_in(key, 102), OWNERS)

    def one_list(list_key):
        return jax.random.permutation(list_key, PB)[:SW].astype(jnp.int32)
    lists = jax.vmap(one_list)(list_keys)
    device_ids = jnp.arange(OWNERS, dtype=jnp.int32)
    weld_idx = device_ids // N_TRANS
    trans_idx = device_ids % N_TRANS
    partner = jnp.bitwise_xor(weld_idx, jnp.left_shift(jnp.int32(1), bits_all)) * N_TRANS + trans_idx
    return (bits_all, lists, partner)


def draw_partner_bit(key, part):
    base_key = key
    bits_all, lists, partner = pairing(base_key)
    return bits_all


def draw_swap_list(key, part):
    base_key = key
    bits_all, lists, partner = pairing(base_key)
    return lists


def draw_targets(key, part):
    base_key = key
    key = jax.random.fold_in(key, 3)
    bits_all, lists, partner = pairing(base_key)
    device_ids = jnp.arange(OWNERS, dtype=jnp.int32)
    dev_keys = jax.random.split(key, OWNERS)

    def one_device(dev_key, device):
        key_a, key_b, key_c = jax.random.split(dev_key, 3)
        others = (jax.random.permutation(key_a, (OWNERS - 1) * CAP)[:PB - CAP] // CAP).astype(jnp.int32)
        others = others + (others >= device).astype(jnp.int32)
        owner_ids = jnp.concatenate([jnp.full((CAP,), device, jnp.int32), others])
        owner_ids = jax.random.permutation(key_b, owner_ids)
        node_ids = jax.random.randint(key_c, (PB,), 0, NBD).astype(jnp.int32)
        return owner_ids * NBD + node_ids
    after = jax.vmap(one_device)(dev_keys, device_ids)
    before = after.at[device_ids[:, None], lists].set(after[partner[:, None], lists[partner]])
    return before.reshape(P_BLOCKS)


def draw_counts(key, part):
    key = jax.random.fold_in(key, 5)
    device_ids = jnp.arange(OWNERS, dtype=jnp.int32)
    weld_idx = device_ids // N_TRANS
    stir_zone = (4 * weld_idx >= N_WELD) & (4 * weld_idx < 3 * N_WELD)
    low_end = jnp.where(stir_zone, 40, 0).astype(jnp.int32)
    high_end = jnp.where(stir_zone, BS + 1, BS // 2 + 1).astype(jnp.int32)
    drawn = jax.random.randint(key, (OWNERS, PB), low_end[:, None], high_end[:, None]).astype(jnp.int32)
    drawn = drawn.at[:, 0].set(BS)
    return drawn.reshape(P_BLOCKS)


def draw_weights(key, part):
    key = jax.random.fold_in(key, 4)

    def one_device(device):
        dev_key = jax.random.fold_in(key, device)
        key_a, key_b = jax.random.split(dev_key, 2)
        spread = jax.random.uniform(key_a, (PB, BS, BS), jnp.float32)
        base = spread * (2.0 / BS)
        slopes = jnp.clip(jax.random.normal(key_b, (PB, BS, 3 * BS), jnp.float32), -4.0, 4.0) / BS
        return jnp.concatenate([base, slopes], -1).astype(jnp.bfloat16)
    return lax.map(one_device, jnp.arange(OWNERS, dtype=jnp.int32)).reshape(P_BLOCKS, BS, 4 * BS)


def levels(rng, extent, cuts, low, largest):
    level = 1.0
    for position, shards_of in cuts:
        steps = jax.random.uniform(jax.random.fold_in(jax.random.fold_in(rng, 6), position), (shards_of,), jnp.float32, low / len(cuts), largest / len(cuts))
        level = level * jnp.repeat(jnp.exp(steps), extent[position] // shards_of).reshape((-1,) + (1,) * (len(extent) - 1 - position))
    return level


def normal_values(own_key, shape, width, bound, cuts=(), kind=jnp.bfloat16):
    entries = jax.random.normal(own_key, shape, jnp.float32) * width
    if len(cuts) > 0:
        entries = levels(own_key, shape, cuts, -0.22, 0.18) * entries
    return jnp.clip(entries, min=-bound, max=bound).astype(kind)


def setup_inputs(seed: int = 0) -> dict:
    splits = jax.random.split(jax.random.key(seed), 9)
    weights = draw_weights(jax.random.fold_in(splits[8], 71), 0)
    particle_state = normal_values(splits[1], (10, PARTICLES), 1.0, 6.0, ((1, 128),), jnp.float32)
    mass = jnp.clip(jnp.exp(math.log(2.0) - 1.3862944 * jax.random.uniform(splits[2], (PARTICLES,), jnp.float32) ** levels(splits[2], (PARTICLES,), ((0, 128),), -0.2, 0.2)), 0.5, 2.0)
    stiffness = jnp.clip(jnp.exp(math.log(10.0) - 2.3025851 * jax.random.uniform(splits[3], (PARTICLES,), jnp.float32) ** levels(splits[3], (PARTICLES,), ((0, 128),), -0.2, 0.2)), 1.0, 10.0)
    targets = draw_targets(jax.random.fold_in(splits[8], 71), 0)
    counts = draw_counts(jax.random.fold_in(splits[8], 71), 0)
    partner_bit = draw_partner_bit(jax.random.fold_in(splits[8], 71), 0)
    swap_list = draw_swap_list(jax.random.fold_in(splits[8], 71), 0)
    return dict(weights=weights, particle_state=particle_state, mass=mass, stiffness=stiffness, targets=targets, counts=counts, partner_bit=partner_bit, swap_list=swap_list)


time_step = 0.25
mass_floor = 0.25
clamp_nodes = 8
sym_index = ((4, 7, 9), (7, 5, 8), (9, 8, 6))
stress_pairs = ((0, 0), (1, 1), (2, 2), (0, 1), (1, 2), (0, 2))


def build_table(masses, current):
    empty_row = jnp.zeros_like(masses)
    first_kind = [masses, masses * current[..., 0, :], masses * current[..., 1, :], masses * current[..., 2, :], empty_row, empty_row, empty_row, masses * current[..., 3, :]]
    kind_list = [jnp.stack(first_kind, -1)]
    for column in range(3):
        terms = [empty_row] * 4 + [-masses * current[..., sym_index[row_k][column], :] for row_k in range(3)] + [empty_row]
        kind_list.append(jnp.stack(terms, -1))
    return jnp.stack(kind_list, -2).astype(jnp.bfloat16)


def grid_update(node_sum):
    msafe = jnp.maximum(node_sum[:, 0], mass_floor)
    velocity = (node_sum[:, 1:4] + time_step * node_sum[:, 4:7]) / msafe[:, None]
    keep_mask = (jnp.arange(node_sum.shape[-1]) >= clamp_nodes).astype(jnp.float32)
    velocity = velocity * keep_mask
    heat_field = node_sum[:, 7] / msafe
    return jnp.concatenate([velocity, heat_field[:, None]], 1).astype(jnp.bfloat16)


def particle_update(current, result, stiff_rows, live_mask):
    new_vel = jnp.moveaxis(result[..., 0, 0:3], -1, -2)
    new_temp = result[..., 0, 3]

    def grad_entry(row_i, col_j):
        return result[..., col_j + 1, row_i]

    strain = [[0.5 * (grad_entry(row_i, col_j) + grad_entry(col_j, row_i)) for col_j in range(3)] for row_i in range(3)]
    trace_sum = strain[0][0] + strain[1][1] + strain[2][2]
    stress_new = []
    for place, (row_i, col_j) in enumerate(stress_pairs):
        extra = trace_sum if row_i == col_j else 0.0
        stress_new.append(current[..., 4 + place, :] + time_step * stiff_rows * (2.0 * strain[row_i][col_j] + extra))
    updated = jnp.concatenate([new_vel, new_temp[..., None, :], jnp.stack(stress_new, -2)], -2)
    return jnp.where(live_mask[..., None, :] > 0, updated, current)


def block_p2g(operands):
    wblock, table = operands
    shaped = wblock.reshape(wblock.shape[0], BS, 4, BS).astype(jnp.float32)
    return jnp.einsum('bpkc,bpkn->bcn', table.astype(jnp.float32), shaped)


def block_g2p(operands):
    fields_b, wblock = operands
    shaped = wblock.reshape(wblock.shape[0], BS, 4, BS).astype(jnp.float32)
    return jnp.einsum('bcn,bpkn->bpkc', fields_b.astype(jnp.float32), shaped)


def reference(weights, particle_state, mass, stiffness, targets, counts, partner_bit, swap_list):
    owners = N_WELD * N_TRANS
    device_ids = jnp.arange(owners, dtype=jnp.int32)
    weld_idx = device_ids // N_TRANS
    trans_idx = device_ids % N_TRANS
    partner = jnp.bitwise_xor(weld_idx, jnp.left_shift(jnp.int32(1), partner_bit)) * N_TRANS + trans_idx

    def swapped(arr):
        source = arr[partner[:, None], swap_list[partner]]
        return arr.at[device_ids[:, None], swap_list].set(source)

    wts = swapped(weights.reshape(owners, PB, BS, 4 * BS))
    current = swapped(particle_state.reshape(10, owners, PB, BS).transpose(1, 2, 0, 3))
    masses = swapped(mass.reshape(owners, PB, BS))
    stiff_rows = swapped(stiffness.reshape(owners, PB, BS))
    target_b = swapped(targets.reshape(owners, PB))
    count_b = swapped(counts.reshape(owners, PB))
    live_mask = (jnp.arange(BS, dtype=jnp.int32)[None, None, :] < count_b[..., None]).astype(jnp.float32)
    fields = None
    for step_idx in range(STEPS):
        table = build_table(masses * live_mask, current)
        partials = lax.map(block_p2g, (wts, table))
        node_sum = jax.ops.segment_sum(partials.reshape(owners * PB, 8 * BS), target_b.reshape(-1), num_segments=NODE_BLOCKS)
        fields = grid_update(node_sum.reshape(NODE_BLOCKS, 8, BS))
        fields_b = fields[target_b]
        result = lax.map(block_g2p, (fields_b, wts))
        current = particle_update(current, result, stiff_rows, live_mask)
    particle_next = current.transpose(2, 0, 1, 3).reshape(10, owners * PB * BS)
    return particle_next, fields.reshape(NODE_BLOCKS, 4 * BS)
```

```python
import functools

import jax
import jax.numpy as jnp
from jax import lax
from jax.experimental import pallas as pl
from jax.experimental.pallas import tpu as pltpu
from jax.sharding import PartitionSpec as P

BS = 64
NBD = 64
PB = 384
SW = 24
N_WELD = 8
N_TRANS = 16
OWN = 128
SLOTS = 4
PAIRS = PB // 2
XPAIRS = SW // 2
ALLP = PAIRS + XPAIRS
ROWS = OWN * 2 * SLOTS
EXT = 512
SWP = 32
CHUNKS = 12
CHP = PAIRS // CHUNKS

f32 = jnp.float32
bf16 = jnp.bfloat16
MESH = pl.DeviceIdType.MESH


def iota(shape, dim):
    return lax.broadcasted_iota(jnp.int32, shape, dim)


def coords(dev):
    return (dev // N_TRANS, dev % N_TRANS)


def dot(lhs, rhs):
    return lax.dot_general(lhs, rhs, (((1,), (0,)), ((), ())), preferred_element_type=f32)


def dot_nt(lhs, rhs):
    return lax.dot_general(lhs, rhs, (((1,), (1,)), ((), ())), preferred_element_type=f32)


def weld_kernel(
    w_hbm, st_ref, mass_ref, stiff_ref, tgt_ref, cnt_ref, bit_ref, swap_ref,
    out_ref, field_ref, xout_ref,
    w_ref, s0_ref, s1_ref, m_ref, sf_ref, pt_ref, pb_ref, fbx_ref, kc_ref, kr_ref,
    sd_ref, at_ref, a_ref, ms_ref,
    send1, recv1, send2, recv2, ans_s, ans_r,
    hs1, hr1, hs2, hr2, fs, fr, xs, xr,
    wsem, asem_s, asem_r, hsem_s, hsem_r,
):
    weld = lax.axis_index("weld")
    trans = lax.axis_index("trans")
    me = weld * N_TRANS + trans
    bar = pltpu.get_barrier_semaphore()

    def chunk_copy(c):
        part = pl.ds(c * CHP * 2, CHP * 2)
        return pltpu.make_async_copy(w_hbm.at[part], w_ref.at[part], wsem.at[c])

    for c in range(CHUNKS):
        chunk_copy(c).start()

    def greet(j, carry):
        pl.semaphore_signal(
            bar, inc=1, device_id=coords(lax.rem(me + j, OWN)), device_id_type=MESH
        )
        return carry

    lax.fori_loop(1, OWN, greet, 0)

    row8 = iota((8, 128), 0)
    lane8 = iota((8, 128), 1)
    lo = lane8 < 64
    lane64 = lane8 % 64

    def all_to_all(src, dst, ph):
        dst[me] = src[me]

        def go(j, carry):
            dev = lax.rem(me + j, OWN)
            pltpu.make_async_remote_copy(
                src.at[dev], dst.at[me], asem_s.at[ph], asem_r.at[ph],
                device_id=coords(dev), device_id_type=MESH,
            ).start()
            return carry

        lax.fori_loop(1, OWN, go, 0)

    def all_to_all_wait(src, dst, ph):
        part = dst.at[pl.ds(0, OWN - 1)]
        pltpu.make_async_copy(part, part, asem_r.at[ph]).wait()
        part = src.at[pl.ds(0, OWN - 1)]
        pltpu.make_async_copy(part, part, asem_s.at[ph]).wait()

    def partner_copies(src, dst, ph):
        out = []
        for bit in range(2):
            step = 1 << bit
            other = weld + step - 2 * step * ((weld // step) % 2)
            out.append(
                pltpu.make_async_remote_copy(
                    src, dst.at[bit], hsem_s.at[ph, bit], hsem_r.at[ph, bit],
                    device_id=(other, trans), device_id_type=MESH,
                )
            )
        return out

    my_bit = bit_ref[0]

    def picked(ref):
        return jnp.where(my_bit == 0, ref[0].astype(f32), ref[1].astype(f32))

    head = row8 < 3
    blk = [lo, jnp.logical_not(lo)]
    zero8 = jnp.zeros((8, 128), f32)

    def scatter_pair(q, s0, s1, mass8):
        t0 = s0 * mass8
        t1 = s1 * (-0.25 * mass8)
        kinds = [t0, t1, pltpu.roll(t1, 3, 0), pltpu.roll(t1, 6, 0)]
        kinds = [t0] + [jnp.where(head, k, 0.0) for k in kinds[1:]]
        tiles = [[jnp.where(blk[b], kinds[k], 0.0) for k in range(4)] for b in range(2)]
        lhs_a = jnp.concatenate(
            [tiles[0][0], tiles[0][1], tiles[1][0], tiles[1][1]], 0
        ).astype(bf16)
        lhs_b = jnp.concatenate(
            [tiles[0][2], tiles[0][3], tiles[1][2], tiles[1][3]], 0
        ).astype(bf16)
        w_pair = w_ref[pl.ds(2 * q, 2)].reshape(128, 256)
        res_a = dot(lhs_a, w_pair[:, 0:128])
        res_b = dot(lhs_b, w_pair[:, 128:256])
        both = []
        for b in range(2):
            both.append(
                jnp.where(lo, res_a[b * 16 : b * 16 + 8], res_a[b * 16 + 8 : b * 16 + 16])
                + jnp.where(lo, res_b[b * 16 : b * 16 + 8], res_b[b * 16 + 8 : b * 16 + 16])
            )
        pt_ref[pl.ds(pl.multiple_of(q * 16, 16), 16), :] = jnp.concatenate(both, 0)

    def first_pair(q, carry):
        lanes = pl.ds(pl.multiple_of(q * 128, 128), 128)

        def row(r):
            return jnp.broadcast_to(st_ref[r : r + 1, lanes], (8, 128))

        s0 = jnp.where(row8 < 4, st_ref[0:8, lanes], jnp.where(row8 == 4, 1.0, 0.0))
        xy, yz = row(7), row(8)
        s1 = jnp.where(row8 == 0, row(4), xy)
        s1 = jnp.where(row8 == 2, row(9), s1)
        s1 = jnp.where(jnp.logical_or(row8 == 3, row8 == 7), yz, s1)
        s1 = jnp.where(row8 == 4, row(6), s1)
        s1 = jnp.where(row8 == 6, row(5), s1)
        many = jnp.where(lo, cnt_ref[2 * q], cnt_ref[2 * q + 1])
        live = lane64 < many
        mass8 = jnp.where(live, jnp.broadcast_to(mass_ref[0:1, lanes], (8, 128)), 0.0)
        stiff8 = jnp.where(live, 0.25 * jnp.broadcast_to(stiff_ref[0:1, lanes], (8, 128)), 0.0)
        s0_ref[q] = s0
        s1_ref[q] = s1
        m_ref[q] = mass8
        sf_ref[q] = stiff8
        scatter_pair(q, s0, s1, mass8)
        return carry

    def next_scatter(q, carry):
        scatter_pair(q, s0_ref[q], s1_ref[q], m_ref[q])
        return carry

    hi = jnp.logical_not(lo)

    def rows_in(*which):
        hit = row8 == which[0]
        for w in which[1:]:
            hit = jnp.logical_or(hit, row8 == w)
        return hit

    def mask(*terms):
        total = zero8
        for value, which, lanes in terms:
            total = total + jnp.where(jnp.logical_and(rows_in(*which), lanes), value, 0.0)
        return total

    f0h0 = [
        mask((1.0, (0,), lo)),
        mask((1.0, (2,), lo)),
        mask((1.0, (1,), lo), (1.0, (5,), hi)),
        mask((1.0, (3,), lo)),
    ]
    f0h1 = [None, None, mask((1.0, (5,), lo)), mask((1.0, (5,), hi))]
    f1h0 = [
        mask((1.0, (1, 5), hi)),
        None,
        mask((2.0, (0,), hi)),
        mask((1.0, (2,), hi)),
    ]
    f1h1 = [
        mask((1.0, (1, 5), lo), (1.0, (3, 7), hi)),
        mask((1.0, (3, 7), lo)),
        mask((2.0, (6,), lo), (1.0, (2,), hi)),
        mask((2.0, (4,), hi)),
    ]
    diag = rows_in(0, 4, 6)

    def combine(masks, vals):
        total = None
        for m, v in zip(masks, vals):
            if m is not None:
                term = m * v
                total = term if total is None else total + term
        return total

    def gather_pair(q, four, place):
        left, right = [], []
        for b in range(2):
            vals = [
                jnp.broadcast_to(
                    four[2 * place + b : 2 * place + b + 1, g * 128 : g * 128 + 128], (8, 128)
                )
                for g in range(4)
            ]
            left += [combine(f0h0, vals), combine(f1h0, vals)]
            right += [combine(f0h1, vals), combine(f1h1, vals)]
        lhs = jnp.concatenate(
            [jnp.concatenate(left, 0).astype(bf16), jnp.concatenate(right, 0).astype(bf16)], 1
        )
        res = dot_nt(lhs, w_ref[pl.ds(2 * q, 2)].reshape(128, 256))
        o0 = jnp.where(lo, res[0:8], res[16:24])
        o1 = jnp.where(lo, res[8:16], res[24:32])
        trace = jnp.where(diag, jnp.broadcast_to(o0[5:6], (8, 128)), 0.0)
        mass8 = m_ref[q]
        s0, s1 = s0_ref[q], s1_ref[q]
        s0 = jnp.where(jnp.logical_and(mass8 > 0.0, row8 < 4), o0, s0)
        s1 = s1 + sf_ref[q] * (o1 + trace)
        return s0, s1, mass8

    def by_fours(one_pair):
        def body(g, carry):
            four = fbx_ref[pl.ds(pl.multiple_of(g * 8, 8), 8), :]
            for place in range(4):
                q = 4 * g + place
                one_pair(q, *gather_pair(q, four, place))
            return carry

        return body

    @by_fours
    def middle_four(q, s0, s1, mass8):
        s0_ref[q] = s0
        s1_ref[q] = s1
        scatter_pair(q, s0, s1, mass8)

    def natural(s0, s1):
        turned = [pltpu.roll(s1, k, 0) for k in (4, 7, 2, 6, 5)]
        top = jnp.where(row8 < 4, s0, turned[0])
        top = jnp.where(row8 == 5, turned[1], top)
        top = jnp.where(row8 == 6, turned[2], top)
        top = jnp.where(row8 == 7, turned[3], top)
        low = jnp.where(row8 == 0, turned[4], turned[1])
        return top, low

    @by_fours
    def last_four(q, s0, s1, mass8):
        top, low = natural(s0, s1)
        lanes = pl.ds(pl.multiple_of(q * 128, 128), 128)
        out_ref[0:8, lanes] = top
        out_ref[8:10, lanes] = low[0:2]

    @by_fours
    def last_extra(q, s0, s1, mass8):
        top, low = natural(s0, s1)
        lanes = pl.ds(pl.multiple_of((q - PAIRS) * 128, 128), 128)
        xs[0:8, lanes] = top
        xs[8:16, lanes] = low

    pt_ref[pl.ds(ALLP * 16, (EXT // 2 - ALLP) * 16), :] = jnp.zeros(
        ((EXT // 2 - ALLP) * 16, 128), f32
    )

    def first_chunk(c, carry):
        chunk_copy(c).wait()
        return lax.fori_loop(
            0, CHP, lambda i, got: first_pair(c * CHP + i, got), carry, unroll=4
        )

    lax.fori_loop(0, CHUNKS, first_chunk, 0)

    def take_extra(i, carry):
        blk_ids = [swap_ref[0, 2 * i + b] for b in range(2)]
        for b in range(2):
            w_ref[PB + 2 * i + b] = w_ref[blk_ids[b]]
        for ref in (s0_ref, s1_ref, m_ref, sf_ref):
            vals = []
            for b in range(2):
                v = ref[lax.div(blk_ids[b], 2)]
                vals.append(jnp.where(lax.rem(blk_ids[b], 2) == b, v, pltpu.roll(v, 64, 1)))
            ref[PAIRS + i] = jnp.where(lo, vals[0], vals[1])
        return carry

    lax.fori_loop(0, XPAIRS, take_extra, 0)
    lax.fori_loop(PAIRS, ALLP, next_scatter, 0, unroll=2)

    def channels(first, count, groups):
        lo_c = iota((count, 128), 1) < 64

        def folded(c):
            v = pt_ref[pl.ds(first * 8 + c, count, stride=8), :]
            return v + pltpu.roll(v, 64, 1)

        parts = [
            jnp.where(lo_c, folded(0), folded(1)),
            jnp.where(lo_c, folded(2), folded(3)),
        ]
        if groups > 2:
            parts.append(folded(4))
        return parts

    tgt = tgt_ref[...].astype(f32)
    own_r = jnp.floor(tgt * (1.0 / NBD))
    node_r = tgt - NBD * own_r + 1.0

    sw_row = iota((SWP, 128), 0)
    sw_col = jnp.full((SWP, 128), -1, jnp.int32)
    for s in range(SW):
        sw_col = jnp.where(sw_row == s, swap_ref[0, s], sw_col)
    flags, own_h, node_h = [], 0.0, 0.0
    for j in range(3):
        hits = (sw_col == iota((SWP, 128), 1) + 128 * j).astype(f32)
        flags.append(jnp.sum(hits, 0, keepdims=True))
        own_h = own_h + jnp.sum(hits * own_r[j : j + 1], 1, keepdims=True)
        node_h = node_h + jnp.sum(hits * node_r[j : j + 1], 1, keepdims=True)
    own_h = jnp.where(sw_row < SW, jnp.broadcast_to(own_h, (SWP, 128)), -1.0)
    node_h = jnp.broadcast_to(node_h, (SWP, 128))

    parts = channels(PB, SWP, 3)
    lo_s = iota((SWP, 128), 1) < 64
    hs1[...] = jnp.concatenate(
        [parts[0], parts[1], jnp.where(lo_s, parts[2], node_h), own_h], 1
    ).astype(bf16)

    pl.semaphore_wait(bar, OWN - 1)
    hand1 = partner_copies(hs1, hr1, 0)
    for c in hand1:
        c.start()

    own_cols = []
    for j in range(3):
        lanes = slice(j * 128, j * 128 + 128)
        own_j = jnp.where(flags[j] > 0.0, -1.0, own_r[j : j + 1])
        own_b = jnp.broadcast_to(own_j, (128, 128))
        kr_ref[:, lanes] = own_b
        own_cols.append(own_b.T)
        node_c = jnp.broadcast_to(node_r[j : j + 1], (128, 128)).T
        parts = channels(j * 128, 128, 3)
        lo_b = iota((128, 128), 1) < 64
        pb_ref[lanes, :] = jnp.concatenate(
            [parts[0], parts[1], jnp.where(lo_b, parts[2], node_c)], 1
        ).astype(bf16)
    pb_ref[PB:EXT, :] = jnp.zeros((EXT - PB, 384), bf16)

    for c in hand1:
        c.wait()
    got = picked(hr1)
    pb_ref[PB : PB + SWP, :] = got[:, 0:384].astype(bf16)
    own_cols.append(jnp.concatenate([got[:, 384:512], jnp.full((96, 128), -1.0, f32)], 0))
    kr_ref[:, PB:EXT] = own_cols[3].T

    before = iota((128, 128), 1) < iota((128, 128), 0)
    for i in range(4):
        count = jnp.zeros((128, 128), f32)
        for j in range(i + 1):
            same = own_cols[i] == kr_ref[:, j * 128 : j * 128 + 128]
            if j == i:
                same = jnp.logical_and(same, before)
            count = count + jnp.where(same, 1.0, 0.0)
        rank = jnp.broadcast_to(jnp.sum(count, 1, keepdims=True), (128, 128))
        key = jnp.where(own_cols[i] >= 0.0, own_cols[i] * SLOTS + rank, -1.0)
        kc_ref[i * 128 : i * 128 + 128, :] = key
    for i in range(4):
        kr_ref[:, i * 128 : i * 128 + 128] = kc_ref[i * 128 : i * 128 + 128, :].T

    def send_rows(c, groups):
        r = iota((128, EXT), 0) + c * 128
        row_key = ((r // 8) * SLOTS + r % SLOTS).astype(f32)
        pick = jnp.where(row_key == kr_ref[...], 1.0, 0.0).astype(bf16)
        res = dot(pick, pb_ref[:, 0 : groups * 128])
        first_half = (iota((128, 128), 0) % 8) < SLOTS
        main = jnp.where(first_half, res[:, 0:128], res[:, 128:256])
        return main.reshape(16, 8, 128), res[:, 256:]

    def fill1(c, carry):
        main, extra = send_rows(c, 3)
        owners = pl.ds(pl.multiple_of(c * 16, 16), 16)
        send1[owners] = jnp.concatenate([main, extra.reshape(16, 8, 128)], 1).astype(bf16)
        return carry

    lax.fori_loop(0, 8, fill1, 0)
    all_to_all(send1, recv1, 0)

    key_lane = iota((EXT, 128), 1)
    for c in range(8):
        lane_key = (((key_lane + c * 128) // 8) * SLOTS + key_lane % SLOTS).astype(f32)
        sd_ref[:, c * 128 : c * 128 + 128] = jnp.where(
            kc_ref[...] == lane_key, 1.0, 0.0
        ).astype(bf16)

    all_to_all_wait(send1, recv1, 0)

    half0 = (iota((128, 128), 0) % 8) < SLOTS
    node_lane = (iota((128, 128), 1) - (NBD - 1)).astype(f32)

    def grid_sum1(c):
        blocks = recv1[c * 16 : c * 16 + 16].astype(f32)
        main = blocks[:, 0:8].reshape(128, 128)
        extra = blocks[:, 8:16].reshape(128, 128)
        hit = jnp.where(
            jnp.logical_and(extra == node_lane, node_lane > 0.0), 1.0, 0.0
        )
        at_ref[c * 128 : c * 128 + 128, :] = hit.astype(bf16)
        hit_t = hit.T.astype(bf16)
        a_ref[:, c * 128 : c * 128 + 128] = hit_t
        rhs = jnp.concatenate(
            [
                jnp.where(half0, main, 0.0),
                jnp.where(half0, 0.0, main),
                jnp.where(half0, extra, 0.0),
            ],
            1,
        ).astype(bf16)
        return dot(hit_t, rhs)

    def grid_sum2(c):
        main = recv2[c * 16 : c * 16 + 16].astype(f32).reshape(128, 128)
        rhs = jnp.concatenate(
            [jnp.where(half0, main, 0.0), jnp.where(half0, 0.0, main)], 1
        ).astype(bf16)
        return dot(a_ref[:, c * 128 : c * 128 + 128], rhs)

    lane_n = iota((NBD, 128), 1)
    keep0 = (lane_n % 64) >= 8
    keep1 = jnp.logical_or(lane_n >= 64, lane_n >= 8)

    def grid_fields(total, msafe):
        vel = jnp.where(keep0, total[NBD:, 0:128] / msafe, 0.0)
        rest = jnp.where(keep1, total[NBD:, 128:256] / msafe, 0.0)
        return jnp.concatenate([vel, rest], 1).astype(bf16)

    def answer(fields, dst):
        rhs = jnp.concatenate([jnp.zeros((NBD, 256), bf16), fields], 0)

        def fill(c, carry):
            rows = pl.ds(pl.multiple_of(c * 128, 128), 128)
            res = dot(at_ref[rows, :], rhs)
            main = jnp.where(half0, res[:, 0:128], res[:, 128:256])
            owners = pl.ds(pl.multiple_of(c * 16, 16), 16)
            dst[owners] = main.reshape(16, 8, 128).astype(bf16)
            return carry

        lax.fori_loop(0, 8, fill, 0)

    def spread(src, ph):
        total = jnp.zeros((EXT, 256), f32)
        for c in range(4):
            main = src[c * 32 : c * 32 + 32].astype(f32).reshape(256, 128)
            first_half = (iota((256, 128), 0) % 8) < SLOTS
            rhs = jnp.concatenate(
                [jnp.where(first_half, main, 0.0), jnp.where(first_half, 0.0, main)], 1
            ).astype(bf16)
            total = total + dot(sd_ref[:, c * 256 : c * 256 + 256], rhs)
        fs[ph] = total[PB : PB + SWP].astype(bf16)
        copies = partner_copies(fs.at[ph], fr.at[ph], 1 + ph)
        for c in copies:
            c.start()
        fbx_ref[0:PB, 0:256] = total[0:PB]
        fbx_ref[0:PB, 256:384] = pltpu.roll(total[0:PB, 0:128], 64, 1)
        fbx_ref[0:PB, 384:512] = pltpu.roll(total[0:PB, 128:256], 64, 1)
        return copies

    def spread_end(copies, ph):
        for c in copies:
            c.wait()
        got = picked(fr.at[ph])
        fbx_ref[PB : PB + SWP, 0:256] = got
        fbx_ref[PB : PB + SWP, 256:384] = pltpu.roll(got[:, 0:128], 64, 1)
        fbx_ref[PB : PB + SWP, 384:512] = pltpu.roll(got[:, 128:256], 64, 1)

    total = grid_sum1(0)
    for c in range(1, 8):
        total = total + grid_sum1(c)
    mass_n = total[NBD:, 256:384]
    msafe = jnp.maximum(jnp.where(lane_n < 64, mass_n, pltpu.roll(mass_n, 64, 1)), 0.25)
    ms_ref[...] = msafe
    answer(grid_fields(total, msafe), ans_s.at[0])
    all_to_all(ans_s.at[0], ans_r.at[0], 1)
    all_to_all_wait(ans_s.at[0], ans_r.at[0], 1)

    copies = spread(ans_r.at[0], 0)
    lax.fori_loop(0, 24, middle_four, 0)
    spread_end(copies, 0)
    lax.fori_loop(PAIRS // 4, ALLP // 4, middle_four, 0)
    hs2[...] = jnp.concatenate(channels(PB, SWP, 2), 1).astype(bf16)
    hand2 = partner_copies(hs2, hr2, 3)
    for c in hand2:
        c.start()
    lax.fori_loop(24, PAIRS // 4, middle_four, 0)
    for j in range(3):
        pb_ref[j * 128 : j * 128 + 128, 0:256] = jnp.concatenate(
            channels(j * 128, 128, 2), 1
        ).astype(bf16)
    for c in hand2:
        c.wait()
    pb_ref[PB : PB + SWP, 0:256] = picked(hr2).astype(bf16)

    def fill2(c, carry):
        main, _ = send_rows(c, 2)
        send2[pl.ds(pl.multiple_of(c * 16, 16), 16)] = main.astype(bf16)
        return carry

    lax.fori_loop(0, 8, fill2, 0)
    all_to_all(send2, recv2, 2)
    all_to_all_wait(send2, recv2, 2)
    total = grid_sum2(0)
    for c in range(1, 8):
        total = total + grid_sum2(c)
    fields = grid_fields(total, ms_ref[...])
    field_ref[...] = fields
    answer(fields, ans_s.at[1])
    all_to_all(ans_s.at[1], ans_r.at[1], 3)
    all_to_all_wait(ans_s.at[1], ans_r.at[1], 3)

    copies = spread(ans_r.at[1], 1)
    lax.fori_loop(0, 24, last_four, 0)
    spread_end(copies, 1)
    lax.fori_loop(PAIRS // 4, ALLP // 4, last_extra, 0)
    hand3 = partner_copies(xs, xr, 4)
    for c in hand3:
        c.start()
    lax.fori_loop(24, PAIRS // 4, last_four, 0)
    for c in hand3:
        c.wait()
    xout_ref[...] = picked(xr)


def weld_call(weights, state, mass, stiff, targets, counts, bit, swap):
    vmem = pl.BlockSpec(memory_space=pltpu.VMEM)
    smem = pl.BlockSpec(memory_space=pltpu.SMEM)
    dma = pltpu.SemaphoreType.DMA
    return pl.pallas_call(
        weld_kernel,
        out_shape=(
            jax.ShapeDtypeStruct((10, PB * BS), f32),
            jax.ShapeDtypeStruct((NBD, 4 * BS), bf16),
            jax.ShapeDtypeStruct((16, XPAIRS * 128), f32),
        ),
        in_specs=[pl.BlockSpec(memory_space=pl.ANY), vmem, vmem, vmem, vmem, smem, smem, smem],
        out_specs=(vmem, vmem, vmem),
        scratch_shapes=[
            pltpu.VMEM((2 * ALLP, BS, 4 * BS), bf16),
            pltpu.VMEM((ALLP, 8, 128), f32),
            pltpu.VMEM((ALLP, 8, 128), f32),
            pltpu.VMEM((ALLP, 8, 128), f32),
            pltpu.VMEM((ALLP, 8, 128), f32),
            pltpu.VMEM((EXT * 8, 128), f32),
            pltpu.VMEM((EXT, 384), bf16),
            pltpu.VMEM((EXT, 512), f32),
            pltpu.VMEM((EXT, 128), f32),
            pltpu.VMEM((128, EXT), f32),
            pltpu.VMEM((EXT, ROWS), bf16),
            pltpu.VMEM((ROWS, 128), bf16),
            pltpu.VMEM((128, ROWS), bf16),
            pltpu.VMEM((NBD, 128), f32),
            pltpu.VMEM((OWN, 16, 128), bf16),
            pltpu.VMEM((OWN, 16, 128), bf16),
            pltpu.VMEM((OWN, 8, 128), bf16),
            pltpu.VMEM((OWN, 8, 128), bf16),
            pltpu.VMEM((2, OWN, 8, 128), bf16),
            pltpu.VMEM((2, OWN, 8, 128), bf16),
            pltpu.VMEM((SWP, 512), bf16),
            pltpu.VMEM((2, SWP, 512), bf16),
            pltpu.VMEM((SWP, 256), bf16),
            pltpu.VMEM((2, SWP, 256), bf16),
            pltpu.VMEM((2, SWP, 256), bf16),
            pltpu.VMEM((2, 2, SWP, 256), bf16),
            pltpu.VMEM((16, XPAIRS * 128), f32),
            pltpu.VMEM((2, 16, XPAIRS * 128), f32),
            dma((CHUNKS,)),
            dma((4,)),
            dma((4,)),
            dma((5, 2)),
            dma((5, 2)),
        ],
        compiler_params=pltpu.CompilerParams(
            collective_id=0, has_side_effects=True, vmem_limit_bytes=56 * 1024 * 1024
        ),
    )(weights, state, mass, stiff, targets, counts, bit, swap)


def place_kernel(own_ref, got_ref, swap_ref, out_ref):
    out_ref[...] = own_ref[...]
    lane = iota((8, 128), 1)

    def place(s, carry):
        blk_id = swap_ref[0, s]
        src = pl.ds(pl.multiple_of((s // 2) * 128, 128), 128)
        dst = pl.ds(pl.multiple_of((blk_id // 2) * 128, 128), 128)
        same = (s % 2) == (blk_id % 2)
        mine = (lane >= 64) == (blk_id % 2 == 1)
        top, low = got_ref[0:8, src], got_ref[8:16, src]
        top = jnp.where(same, top, pltpu.roll(top, 64, 1))
        low = jnp.where(same, low, pltpu.roll(low, 64, 1))
        out_ref[0:8, dst] = jnp.where(mine, top, out_ref[0:8, dst])
        out_ref[8:10, dst] = jnp.where(mine[0:2], low[0:2], out_ref[8:10, dst])
        return carry

    lax.fori_loop(0, SW, place, 0)


def place_call(own, got, swap):
    vmem = pl.BlockSpec(memory_space=pltpu.VMEM)
    return pl.pallas_call(
        place_kernel,
        out_shape=jax.ShapeDtypeStruct((10, PB * BS), f32),
        in_specs=[vmem, vmem, pl.BlockSpec(memory_space=pltpu.SMEM)],
        out_specs=vmem,
        compiler_params=pltpu.CompilerParams(vmem_limit_bytes=32 * 1024 * 1024),
    )(own, got, swap)


def shards(weights, particle_state, mass, stiffness, targets, counts, partner_bit, swap_list):
    own, fields, got = weld_call(
        weights,
        particle_state,
        mass.reshape(1, PB * BS),
        stiffness.reshape(1, PB * BS),
        targets.reshape(3, 128),
        counts,
        partner_bit,
        swap_list,
    )
    return place_call(own, got, swap_list), fields


def solution(mesh):
    both = ("weld", "trans")
    in_specs = (
        P(both, None, None),
        P(None, both),
        P(both),
        P(both),
        P(both),
        P(both),
        P(both),
        P(both, None),
    )
    out_specs = (P(None, both), P(both, None))
    return jax.shard_map(shards, mesh=mesh, in_specs=in_specs, out_specs=out_specs, check_vma=False)
```

```python
import functools

import jax
import jax.numpy as jnp
from jax import lax
from jax.experimental import pallas as pl
from jax.experimental.pallas import tpu as pltpu
from jax.sharding import PartitionSpec as P

BS = 64
NBD = 64
PB = 384
SW = 24
N_WELD = 8
N_TRANS = 16
OWN = 128
SLOTS = 4
PAIRS = PB // 2
XPAIRS = SW // 2
ALLP = PAIRS + XPAIRS
ROWS = OWN * 2 * SLOTS
EXT = 512
SWP = 32
GROUP = 12
CHP = 12
CHUNKS = PAIRS // CHP
NAT = PAIRS // GROUP
EARLY = CHUNKS * 2 // 3

f32 = jnp.float32
bf16 = jnp.bfloat16
MESH = pl.DeviceIdType.MESH


def iota(shape, dim):
    return lax.broadcasted_iota(jnp.int32, shape, dim)


def coords(dev):
    return (dev // N_TRANS, dev % N_TRANS)


def dot(lhs, rhs):
    return lax.dot_general(lhs, rhs, (((1,), (0,)), ((), ())), preferred_element_type=f32)


def dot_nt(lhs, rhs):
    return lax.dot_general(lhs, rhs, (((1,), (1,)), ((), ())), preferred_element_type=f32)


def weld_kernel(
    w_hbm, st_ref, mass_ref, stiff_ref, tgt_ref, cnt_ref, bit_ref, swap_ref,
    out_ref, field_ref, xout_ref,
    w_ref, s0_ref, s1_ref, m0_ref, m1_ref, f0_ref, f1_ref, pt_ref, pb_ref, fbx_ref, kc_ref, kr_ref,
    sd_ref, at_ref, a_ref, ms_ref,
    send1, recv1, send2, recv2, ans_s, ans_r,
    hs1, hr1, hs2, hr2, fs, fr, xs, xr,
    wsem, asem_s, asem_r, hsem_s, hsem_r,
):
    weld = lax.axis_index("weld")
    trans = lax.axis_index("trans")
    me = weld * N_TRANS + trans
    bar = pltpu.get_barrier_semaphore()

    def chunk_copy(c):
        part = pl.ds(c * CHP * 2, CHP * 2)
        return pltpu.make_async_copy(w_hbm.at[part], w_ref.at[part], wsem.at[c])

    for c in range(CHUNKS):
        chunk_copy(c).start()

    def greet(j, carry):
        pl.semaphore_signal(
            bar, inc=1, device_id=coords(lax.rem(me + j, OWN)), device_id_type=MESH
        )
        return carry

    lax.fori_loop(1, OWN, greet, 0)

    row8 = iota((8, 128), 0)
    lane8 = iota((8, 128), 1)
    lo = lane8 < 64
    lane64 = lane8 % 64
    gap = jnp.logical_or(row8 == 3, row8 == 4)

    def all_to_all(fill, src, dst, ph):
        def row(i, carry):
            w = lax.rem(weld + i, N_WELD)
            fill(w)

            def go(j, inner):
                t = lax.rem(trans + j, N_TRANS)
                dev = w * N_TRANS + t

                @pl.when(dev != me)
                def _():
                    pltpu.make_async_remote_copy(
                        src.at[dev], dst.at[me], asem_s.at[ph], asem_r.at[ph],
                        device_id=(w, t), device_id_type=MESH,
                    ).start()

                return inner

            lax.fori_loop(0, N_TRANS, go, 0)
            return carry

        lax.fori_loop(0, N_WELD, row, 0)
        dst[me] = src[me]

    def all_to_all_wait(src, dst, ph):
        part = dst.at[pl.ds(0, OWN - 1)]
        pltpu.make_async_copy(part, part, asem_r.at[ph]).wait()
        part = src.at[pl.ds(0, OWN - 1)]
        pltpu.make_async_copy(part, part, asem_s.at[ph]).wait()

    def partner_copies(src, dst, ph):
        out = []
        for bit in range(2):
            step = 1 << bit
            other = weld + step - 2 * step * ((weld // step) % 2)
            out.append(
                pltpu.make_async_remote_copy(
                    src, dst.at[bit], hsem_s.at[ph, bit], hsem_r.at[ph, bit],
                    device_id=(other, trans), device_id_type=MESH,
                )
            )
        return out

    my_bit = bit_ref[0]

    def picked(ref):
        return jnp.where(my_bit == 0, ref[0].astype(f32), ref[1].astype(f32))

    def scatter_pair(q, s0, s1):
        t0, t1 = s0 * m0_ref[q], s1 * m1_ref[q]
        lhs = [
            jnp.concatenate([jnp.where(lo, t, 0.0), jnp.where(lo, 0.0, t)], 0).astype(bf16)
            for t in (t0, t1)
        ]
        w_pair = w_ref[pl.ds(2 * q, 2)].reshape(128, 256)
        return dot(lhs[0], w_pair[:, 0:128]) + dot(lhs[1], w_pair[:, 128:256])

    def scatter_put(q, res):
        pt_ref[pl.ds(pl.multiple_of(q * 16, 16), 16), :] = res

    def build_pair(q, carry):
        lanes = pl.ds(pl.multiple_of(q * 128, 128), 128)

        def row(r):
            return jnp.broadcast_to(st_ref[r : r + 1, lanes], (8, 128))

        xy, yz, xz = row(7), row(8), row(9)
        s0 = jnp.where(row8 < 4, st_ref[0:8, lanes], jnp.where(row8 == 4, 1.0, xz))
        s0 = jnp.where(row8 == 5, row(4), jnp.where(row8 == 6, xy, s0))
        s1 = jnp.where(row8 == 0, xy, jnp.where(row8 == 1, row(5), yz))
        s1 = jnp.where(row8 == 5, xz, jnp.where(row8 == 7, row(6), s1))
        s1 = jnp.where(gap, 0.0, s1)
        many = jnp.where(lo, cnt_ref[2 * q], cnt_ref[2 * q + 1])
        live = lane64 < many
        mass8 = jnp.where(live, jnp.broadcast_to(mass_ref[0:1, lanes], (8, 128)), 0.0)
        stiff8 = jnp.where(live, 0.25 * jnp.broadcast_to(stiff_ref[0:1, lanes], (8, 128)), 0.0)
        s0_ref[q] = s0
        s1_ref[q] = s1
        m0_ref[q] = jnp.where(row8 < 5, mass8, -0.25 * mass8)
        m1_ref[q] = -0.25 * mass8
        f0_ref[q] = jnp.where(row8 < 5, 0.0, stiff8)
        f1_ref[q] = jnp.where(gap, 0.0, stiff8)
        return carry

    def scatter_group(g, carry):
        group = [GROUP * g + p for p in range(GROUP)]
        sums = [scatter_pair(q, s0_ref[q], s1_ref[q]) for q in group]
        for q, res in zip(group, sums):
            scatter_put(q, res)
        return carry

    hi = jnp.logical_not(lo)

    def rows_in(*which):
        hit = row8 == which[0]
        for w in which[1:]:
            hit = jnp.logical_or(hit, row8 == w)
        return hit

    def mask(*terms):
        total = jnp.zeros((8, 128), f32)
        for value, which, lanes in terms:
            total = total + jnp.where(jnp.logical_and(rows_in(*which), lanes), value, 0.0)
        return total

    f0h0 = [
        mask((1.0, (0,), lo), (1.0, (6,), hi)),
        mask((1.0, (2,), lo)),
        mask((1.0, (1,), lo), (2.0, (5,), hi)),
        mask((1.0, (3,), lo), (1.0, (7,), hi)),
    ]
    f0h1 = [mask((1.0, (6,), lo)), None, mask((1.0, (7,), hi)), None]
    f1h0 = [
        mask((1.0, (0,), hi)),
        None,
        mask((1.0, (3,), hi)),
        mask((1.0, (5,), hi)),
    ]
    f1h1 = [
        mask((1.0, (0,), lo), (1.0, (2, 6), hi)),
        mask((1.0, (2, 6), lo)),
        mask((2.0, (1,), lo), (1.0, (3,), lo), (1.0, (5,), hi)),
        mask((1.0, (3,), hi), (2.0, (7,), hi)),
    ]

    def combine(masks, vals):
        total = None
        for m, v in zip(masks, vals):
            if m is not None:
                term = m * v
                total = term if total is None else total + term
        return total

    def gather_pair(q):
        left, right = [], []
        for b in range(2):
            vals = [
                jnp.broadcast_to(fbx_ref[2 * q + b, g : g + 1, :], (8, 128)) for g in range(4)
            ]
            left += [combine(f0h0, vals), combine(f1h0, vals)]
            right += [combine(f0h1, vals), combine(f1h1, vals)]
        lhs = jnp.concatenate(
            [jnp.concatenate(left, 0).astype(bf16), jnp.concatenate(right, 0).astype(bf16)], 1
        )
        res = dot_nt(lhs, w_ref[pl.ds(2 * q, 2)].reshape(128, 256))
        o0 = jnp.where(lo, res[0:8], res[16:24])
        o1 = jnp.where(lo, res[8:16], res[24:32])
        trace = jnp.broadcast_to(o1[3:4], (8, 128))
        s0, s1 = s0_ref[q], s1_ref[q]
        fresh = jnp.logical_and(m0_ref[q] > 0.0, row8 < 4)
        s0 = jnp.where(fresh, o0, s0 + f0_ref[q] * jnp.where(row8 == 5, o0 + trace, o0))
        s1 = s1 + f1_ref[q] * jnp.where(
            jnp.logical_or(row8 == 1, row8 == 7), o1 + trace, o1
        )
        return s0, s1

    def middle_group(g, carry):
        group = [GROUP * g + p for p in range(GROUP)]
        state = [gather_pair(q) for q in group]
        sums = [scatter_pair(q, *st) for q, st in zip(group, state)]
        for q, (s0, s1), res in zip(group, state, sums):
            s0_ref[q] = s0
            s1_ref[q] = s1
            scatter_put(q, res)
        return carry

    def natural(s0, s1):
        top = jnp.where(row8 < 4, s0, pltpu.roll(s0, 7, 0))
        top = jnp.where(row8 == 5, pltpu.roll(s1, 4, 0), top)
        top = jnp.where(row8 == 6, pltpu.roll(s1, 7, 0), top)
        top = jnp.where(row8 == 7, pltpu.roll(s0, 1, 0), top)
        low = jnp.where(row8 == 0, pltpu.roll(s1, 6, 0), pltpu.roll(s0, 2, 0))
        return top, low

    def last_tiles(first, dst):
        def body(g, carry):
            group = [GROUP * g + p for p in range(GROUP)]
            state = [natural(*gather_pair(q)) for q in group]
            for q, (top, low) in zip(group, state):
                lanes = pl.ds(pl.multiple_of((q - first) * 128, 128), 128)
                dst[0:8, lanes] = top
                dst[8:10, lanes] = low[0:2]
            return carry

        return body

    last_group = last_tiles(0, out_ref)
    last_extra = last_tiles(PAIRS, xs)

    pt_ref[pl.ds(ALLP * 16, (EXT // 2 - ALLP) * 16), :] = jnp.zeros(
        ((EXT // 2 - ALLP) * 16, 128), f32
    )

    def first_chunk(c, carry):
        chunk_copy(c).wait()
        return lax.fori_loop(
            0, CHP // GROUP, lambda i, got: scatter_group(c * (CHP // GROUP) + i, got), carry
        )

    lax.fori_loop(0, PAIRS, build_pair, 0, unroll=4)
    lax.fori_loop(0, EARLY, first_chunk, 0)
    for c in range(EARLY, CHUNKS):
        chunk_copy(c).wait()

    def take_extra(i, carry):
        blk_ids = [swap_ref[0, 2 * i + b] for b in range(2)]
        for b in range(2):
            w_ref[PB + 2 * i + b] = w_ref[blk_ids[b]]
        for ref in (s0_ref, s1_ref, m0_ref, m1_ref, f0_ref, f1_ref):
            vals = []
            for b in range(2):
                v = ref[lax.div(blk_ids[b], 2)]
                vals.append(jnp.where(lax.rem(blk_ids[b], 2) == b, v, pltpu.roll(v, 64, 1)))
            ref[PAIRS + i] = jnp.where(lo, vals[0], vals[1])
        return carry

    lax.fori_loop(0, XPAIRS, take_extra, 0)
    lax.fori_loop(NAT, ALLP // GROUP, scatter_group, 0)

    def channels(first, count, groups):
        lo_c = iota((count, 128), 1) < 64
        v = [pt_ref[pl.ds(first * 8 + c, count, stride=8), :] for c in range(8)]
        parts = [
            jnp.where(lo_c, v[0], v[6]) + pltpu.roll(jnp.where(lo_c, v[1], v[5]), 64, 1),
            jnp.where(lo_c, v[2], 0.0) + pltpu.roll(jnp.where(lo_c, v[3], v[7]), 64, 1),
        ]
        if groups > 2:
            parts.append(v[4])
        return parts

    tgt = tgt_ref[...].astype(f32)
    own_r = jnp.floor(tgt * (1.0 / NBD))
    node_r = tgt - NBD * own_r + 1.0

    sw_row = iota((SWP, 128), 0)
    sw_col = jnp.full((SWP, 128), -1, jnp.int32)
    for s in range(SW):
        sw_col = jnp.where(sw_row == s, swap_ref[0, s], sw_col)
    flags, own_h, node_h = [], 0.0, 0.0
    for j in range(3):
        hits = (sw_col == iota((SWP, 128), 1) + 128 * j).astype(f32)
        flags.append(jnp.sum(hits, 0, keepdims=True))
        own_h = own_h + jnp.sum(hits * own_r[j : j + 1], 1, keepdims=True)
        node_h = node_h + jnp.sum(hits * node_r[j : j + 1], 1, keepdims=True)
    own_h = jnp.where(sw_row < SW, jnp.broadcast_to(own_h, (SWP, 128)), -1.0)
    node_h = jnp.broadcast_to(node_h, (SWP, 128))

    parts = channels(PB, SWP, 3)
    lo_s = iota((SWP, 128), 1) < 64
    hs1[...] = jnp.concatenate(
        [parts[0], parts[1], jnp.where(lo_s, parts[2], node_h), own_h], 1
    ).astype(bf16)

    pl.semaphore_wait(bar, OWN - 1)
    hand1 = partner_copies(hs1, hr1, 0)
    for c in hand1:
        c.start()
    lax.fori_loop(EARLY * CHP // GROUP, NAT, scatter_group, 0)

    own_cols = []
    for j in range(3):
        lanes = slice(j * 128, j * 128 + 128)
        own_j = jnp.where(flags[j] > 0.0, -1.0, own_r[j : j + 1])
        own_b = jnp.broadcast_to(own_j, (128, 128))
        kr_ref[:, lanes] = own_b
        own_cols.append(own_b.T)
        node_c = jnp.broadcast_to(node_r[j : j + 1], (128, 128)).T
        parts = channels(j * 128, 128, 3)
        lo_b = iota((128, 128), 1) < 64
        pb_ref[lanes, :] = jnp.concatenate(
            [parts[0], parts[1], jnp.where(lo_b, parts[2], node_c)], 1
        ).astype(bf16)
    pb_ref[PB:EXT, :] = jnp.zeros((EXT - PB, 384), bf16)

    for c in hand1:
        c.wait()
    got = picked(hr1)
    pb_ref[PB : PB + SWP, :] = got[:, 0:384].astype(bf16)
    own_cols.append(jnp.concatenate([got[:, 384:512], jnp.full((96, 128), -1.0, f32)], 0))
    kr_ref[:, PB:EXT] = own_cols[3].T

    before = iota((128, 128), 1) < iota((128, 128), 0)
    for i in range(4):
        count = jnp.zeros((128, 128), f32)
        for j in range(i + 1):
            same = own_cols[i] == kr_ref[:, j * 128 : j * 128 + 128]
            if j == i:
                same = jnp.logical_and(same, before)
            count = count + jnp.where(same, 1.0, 0.0)
        rank = jnp.broadcast_to(jnp.sum(count, 1, keepdims=True), (128, 128))
        key = jnp.where(own_cols[i] >= 0.0, own_cols[i] * SLOTS + rank, -1.0)
        kc_ref[i * 128 : i * 128 + 128, :] = key
    for i in range(4):
        kr_ref[:, i * 128 : i * 128 + 128] = kc_ref[i * 128 : i * 128 + 128, :].T

    def send_rows(c, groups):
        r = iota((128, EXT), 0) + c * 128
        row_key = ((r // 8) * SLOTS + r % SLOTS).astype(f32)
        pick = jnp.where(row_key == kr_ref[...], 1.0, 0.0).astype(bf16)
        res = dot(pick, pb_ref[:, 0 : groups * 128])
        first_half = (iota((128, 128), 0) % 8) < SLOTS
        main = jnp.where(first_half, res[:, 0:128], res[:, 128:256])
        return main.reshape(16, 8, 128), res[:, 256:]

    def fill1(c):
        main, extra = send_rows(c, 3)
        owners = pl.ds(pl.multiple_of(c * 16, 16), 16)
        send1[owners] = jnp.concatenate([main, extra.reshape(16, 8, 128)], 1).astype(bf16)

    all_to_all(fill1, send1, recv1, 0)

    key_lane = iota((EXT, 128), 1)
    for c in range(8):
        lane_key = (((key_lane + c * 128) // 8) * SLOTS + key_lane % SLOTS).astype(f32)
        sd_ref[:, c * 128 : c * 128 + 128] = jnp.where(
            kc_ref[...] == lane_key, 1.0, 0.0
        ).astype(bf16)

    all_to_all_wait(send1, recv1, 0)

    half0 = (iota((128, 128), 0) % 8) < SLOTS
    node_lane = (iota((128, 128), 1) - (NBD - 1)).astype(f32)

    def grid_sum1(c):
        blocks = recv1[c * 16 : c * 16 + 16].astype(f32)
        main = blocks[:, 0:8].reshape(128, 128)
        extra = blocks[:, 8:16].reshape(128, 128)
        hit = jnp.where(
            jnp.logical_and(extra == node_lane, node_lane > 0.0), 1.0, 0.0
        )
        at_ref[c * 128 : c * 128 + 128, :] = hit.astype(bf16)
        hit_t = hit.T.astype(bf16)
        a_ref[:, c * 128 : c * 128 + 128] = hit_t
        rhs = jnp.concatenate(
            [
                jnp.where(half0, main, 0.0),
                jnp.where(half0, 0.0, main),
                jnp.where(half0, extra, 0.0),
            ],
            1,
        ).astype(bf16)
        return dot(hit_t, rhs)

    def grid_sum2(c):
        main = recv2[c * 16 : c * 16 + 16].astype(f32).reshape(128, 128)
        rhs = jnp.concatenate(
            [jnp.where(half0, main, 0.0), jnp.where(half0, 0.0, main)], 1
        ).astype(bf16)
        return dot(a_ref[:, c * 128 : c * 128 + 128], rhs)

    lane_n = iota((NBD, 128), 1)
    keep0 = (lane_n % 64) >= 8
    keep1 = jnp.logical_or(lane_n >= 64, lane_n >= 8)

    def grid_fields(total, msafe):
        vel = jnp.where(keep0, total[NBD:, 0:128] / msafe, 0.0)
        rest = jnp.where(keep1, total[NBD:, 128:256] / msafe, 0.0)
        return jnp.concatenate([vel, rest], 1).astype(bf16)

    def answer(fields, ph):
        rhs = jnp.concatenate([jnp.zeros((NBD, 256), bf16), fields], 0)

        def fill(c):
            rows = pl.ds(pl.multiple_of(c * 128, 128), 128)
            res = dot(at_ref[rows, :], rhs)
            main = jnp.where(half0, res[:, 0:128], res[:, 128:256])
            owners = pl.ds(pl.multiple_of(c * 16, 16), 16)
            ans_s[ph, owners] = main.reshape(16, 8, 128).astype(bf16)

        all_to_all(fill, ans_s.at[ph], ans_r.at[ph], 1 + 2 * ph)

    def put_fields(first, count, fields):
        flat = fbx_ref.reshape(EXT * 8, 128)
        a, b = fields[0:count, 0:128], fields[0:count, 128:256]
        for g, val in enumerate((a, b, pltpu.roll(a, 64, 1), pltpu.roll(b, 64, 1))):
            flat[pl.ds(first * 8 + g, count, stride=8), :] = val

    def spread(src, ph):
        total = jnp.zeros((EXT, 256), f32)
        for c in range(4):
            main = src[c * 32 : c * 32 + 32].astype(f32).reshape(256, 128)
            first_half = (iota((256, 128), 0) % 8) < SLOTS
            rhs = jnp.concatenate(
                [jnp.where(first_half, main, 0.0), jnp.where(first_half, 0.0, main)], 1
            ).astype(bf16)
            total = total + dot(sd_ref[:, c * 256 : c * 256 + 256], rhs)
        fs[ph] = total[PB : PB + SWP].astype(bf16)
        copies = partner_copies(fs.at[ph], fr.at[ph], 1 + ph)
        for c in copies:
            c.start()
        put_fields(0, PB, total)
        return copies

    def spread_end(copies, ph):
        for c in copies:
            c.wait()
        got = picked(fr.at[ph])
        put_fields(PB, SWP, got)

    total = grid_sum1(0)
    for c in range(1, 8):
        total = total + grid_sum1(c)
    mass_n = total[NBD:, 256:384]
    msafe = jnp.maximum(jnp.where(lane_n < 64, mass_n, pltpu.roll(mass_n, 64, 1)), 0.25)
    ms_ref[...] = msafe
    answer(grid_fields(total, msafe), 0)
    all_to_all_wait(ans_s.at[0], ans_r.at[0], 1)

    copies = spread(ans_r.at[0], 0)
    lax.fori_loop(0, NAT // 2, middle_group, 0)
    spread_end(copies, 0)
    lax.fori_loop(NAT, ALLP // GROUP, middle_group, 0)
    hs2[...] = jnp.concatenate(channels(PB, SWP, 2), 1).astype(bf16)
    hand2 = partner_copies(hs2, hr2, 3)
    for c in hand2:
        c.start()
    lax.fori_loop(NAT // 2, NAT, middle_group, 0)
    for j in range(3):
        pb_ref[j * 128 : j * 128 + 128, 0:256] = jnp.concatenate(
            channels(j * 128, 128, 2), 1
        ).astype(bf16)
    for c in hand2:
        c.wait()
    pb_ref[PB : PB + SWP, 0:256] = picked(hr2).astype(bf16)

    def fill2(c):
        main, _ = send_rows(c, 2)
        send2[pl.ds(pl.multiple_of(c * 16, 16), 16)] = main.astype(bf16)

    all_to_all(fill2, send2, recv2, 2)
    all_to_all_wait(send2, recv2, 2)
    total = grid_sum2(0)
    for c in range(1, 8):
        total = total + grid_sum2(c)
    fields = grid_fields(total, ms_ref[...])
    field_ref[...] = fields
    answer(fields, 1)
    all_to_all_wait(ans_s.at[1], ans_r.at[1], 3)

    copies = spread(ans_r.at[1], 1)
    lax.fori_loop(0, NAT // 2, last_group, 0)
    spread_end(copies, 1)
    lax.fori_loop(NAT, ALLP // GROUP, last_extra, 0)
    hand3 = partner_copies(xs, xr, 4)
    for c in hand3:
        c.start()
    lax.fori_loop(NAT // 2, NAT, last_group, 0)
    for c in hand3:
        c.wait()
    xout_ref[...] = picked(xr)


def weld_call(weights, state, mass, stiff, targets, counts, bit, swap):
    vmem = pl.BlockSpec(memory_space=pltpu.VMEM)
    smem = pl.BlockSpec(memory_space=pltpu.SMEM)
    dma = pltpu.SemaphoreType.DMA
    return pl.pallas_call(
        weld_kernel,
        out_shape=(
            jax.ShapeDtypeStruct((10, PB * BS), f32),
            jax.ShapeDtypeStruct((NBD, 4 * BS), bf16),
            jax.ShapeDtypeStruct((16, XPAIRS * 128), f32),
        ),
        in_specs=[pl.BlockSpec(memory_space=pl.ANY), vmem, vmem, vmem, vmem, smem, smem, smem],
        out_specs=(vmem, vmem, vmem),
        scratch_shapes=[
            pltpu.VMEM((2 * ALLP, BS, 4 * BS), bf16),
            pltpu.VMEM((ALLP, 8, 128), f32),
            pltpu.VMEM((ALLP, 8, 128), f32),
            pltpu.VMEM((ALLP, 8, 128), f32),
            pltpu.VMEM((ALLP, 8, 128), f32),
            pltpu.VMEM((ALLP, 8, 128), f32),
            pltpu.VMEM((ALLP, 8, 128), f32),
            pltpu.VMEM((EXT * 8, 128), f32),
            pltpu.VMEM((EXT, 384), bf16),
            pltpu.VMEM((EXT, 8, 128), f32),
            pltpu.VMEM((EXT, 128), f32),
            pltpu.VMEM((128, EXT), f32),
            pltpu.VMEM((EXT, ROWS), bf16),
            pltpu.VMEM((ROWS, 128), bf16),
            pltpu.VMEM((128, ROWS), bf16),
            pltpu.VMEM((NBD, 128), f32),
            pltpu.VMEM((OWN, 16, 128), bf16),
            pltpu.VMEM((OWN, 16, 128), bf16),
            pltpu.VMEM((OWN, 8, 128), bf16),
            pltpu.VMEM((OWN, 8, 128), bf16),
            pltpu.VMEM((2, OWN, 8, 128), bf16),
            pltpu.VMEM((2, OWN, 8, 128), bf16),
            pltpu.VMEM((SWP, 512), bf16),
            pltpu.VMEM((2, SWP, 512), bf16),
            pltpu.VMEM((SWP, 256), bf16),
            pltpu.VMEM((2, SWP, 256), bf16),
            pltpu.VMEM((2, SWP, 256), bf16),
            pltpu.VMEM((2, 2, SWP, 256), bf16),
            pltpu.VMEM((16, XPAIRS * 128), f32),
            pltpu.VMEM((2, 16, XPAIRS * 128), f32),
            dma((CHUNKS,)),
            dma((4,)),
            dma((4,)),
            dma((5, 2)),
            dma((5, 2)),
        ],
        compiler_params=pltpu.CompilerParams(
            collective_id=0, has_side_effects=True, vmem_limit_bytes=56 * 1024 * 1024
        ),
    )(weights, state, mass, stiff, targets, counts, bit, swap)


def place_kernel(own_ref, got_ref, swap_ref, out_ref):
    out_ref[...] = own_ref[...]
    lane = iota((8, 128), 1)

    def place(s, carry):
        blk_id = swap_ref[0, s]
        src = pl.ds(pl.multiple_of((s // 2) * 128, 128), 128)
        dst = pl.ds(pl.multiple_of((blk_id // 2) * 128, 128), 128)
        same = (s % 2) == (blk_id % 2)
        mine = (lane >= 64) == (blk_id % 2 == 1)
        top, low = got_ref[0:8, src], got_ref[8:16, src]
        top = jnp.where(same, top, pltpu.roll(top, 64, 1))
        low = jnp.where(same, low, pltpu.roll(low, 64, 1))
        out_ref[0:8, dst] = jnp.where(mine, top, out_ref[0:8, dst])
        out_ref[8:10, dst] = jnp.where(mine[0:2], low[0:2], out_ref[8:10, dst])
        return carry

    lax.fori_loop(0, SW, place, 0)


def place_call(own, got, swap):
    vmem = pl.BlockSpec(memory_space=pltpu.VMEM)
    return pl.pallas_call(
        place_kernel,
        out_shape=jax.ShapeDtypeStruct((10, PB * BS), f32),
        in_specs=[vmem, vmem, pl.BlockSpec(memory_space=pltpu.SMEM)],
        out_specs=vmem,
        compiler_params=pltpu.CompilerParams(vmem_limit_bytes=32 * 1024 * 1024),
    )(own, got, swap)


def shards(weights, particle_state, mass, stiffness, targets, counts, partner_bit, swap_list):
    own, fields, got = weld_call(
        weights,
        particle_state,
        mass.reshape(1, PB * BS),
        stiffness.reshape(1, PB * BS),
        targets.reshape(3, 128),
        counts,
        partner_bit,
        swap_list,
    )
    return place_call(own, got, swap_list), fields


def solution(mesh):
    both = ("weld", "trans")
    in_specs = (
        P(both, None, None),
        P(None, both),
        P(both),
        P(both),
        P(both),
        P(both),
        P(both),
        P(both, None),
    )
    out_specs = (P(None, both), P(both, None))
    return jax.shard_map(shards, mesh=mesh, in_specs=in_specs, out_specs=out_specs, check_vma=False)
```

```python
import functools

import jax
import jax.numpy as jnp
from jax import lax
from jax.experimental import pallas as pl
from jax.experimental.pallas import tpu as pltpu
from jax.sharding import PartitionSpec as P

BS = 64
NBD = 64
PB = 384
SW = 24
N_WELD = 8
N_TRANS = 16
OWN = 128
SLOTS = 4
PAIRS = PB // 2
XPAIRS = SW // 2
ALLP = PAIRS + XPAIRS
ROWS = OWN * 2 * SLOTS
EXT = 512
SWP = 32
GROUP = 12
CHP = 12
CHUNKS = PAIRS // CHP
NAT = PAIRS // GROUP
EARLY = CHUNKS * 2 // 3

f32 = jnp.float32
bf16 = jnp.bfloat16
MESH = pl.DeviceIdType.MESH


def iota(shape, dim):
    return lax.broadcasted_iota(jnp.int32, shape, dim)


def coords(dev):
    return (dev // N_TRANS, dev % N_TRANS)


def dot(lhs, rhs):
    return lax.dot_general(lhs, rhs, (((1,), (0,)), ((), ())), preferred_element_type=f32)


def dot_nt(lhs, rhs):
    return lax.dot_general(lhs, rhs, (((1,), (1,)), ((), ())), preferred_element_type=f32)


def weld_kernel(
    w_hbm, st_ref, mass_ref, stiff_ref, tgt_ref, cnt_ref, bit_ref, swap_ref,
    out_ref, field_ref, xout_ref,
    w_ref, s0_ref, s1_ref, m0_ref, m1_ref, f0_ref, f1_ref, pt_ref, pb_ref, fbx_ref, kc_ref, kr_ref,
    sd_ref, at_ref, a_ref, ms_ref,
    send1, recv1, send2, recv2, ans_s, ans_r,
    hs1, hr1, hs2, hr2, fs, fr, xs, xr,
    wsem, asem_s, asem_r, hsem_s, hsem_r,
):
    weld = lax.axis_index("weld")
    trans = lax.axis_index("trans")
    me = weld * N_TRANS + trans
    bar = pltpu.get_barrier_semaphore()

    def chunk_copy(c):
        part = pl.ds(c * CHP * 2, CHP * 2)
        return pltpu.make_async_copy(w_hbm.at[part], w_ref.at[part], wsem.at[c])

    for c in range(CHUNKS):
        chunk_copy(c).start()

    def greet(j, carry):
        pl.semaphore_signal(
            bar, inc=1, device_id=coords(lax.rem(me + j, OWN)), device_id_type=MESH
        )
        return carry

    lax.fori_loop(1, OWN, greet, 0)

    row8 = iota((8, 128), 0)
    lane8 = iota((8, 128), 1)
    lo = lane8 < 64
    lane64 = lane8 % 64
    gap = jnp.logical_or(row8 == 3, row8 == 4)

    def all_to_all(fill, src, dst, ph):
        def row(i, carry):
            w = lax.rem(weld + N_WELD // 2 + i, N_WELD)
            fill(w)

            def go(j, inner):
                t = lax.rem(trans + N_TRANS // 2 + j, N_TRANS)
                dev = w * N_TRANS + t

                @pl.when(dev != me)
                def _():
                    pltpu.make_async_remote_copy(
                        src.at[dev], dst.at[me], asem_s.at[ph], asem_r.at[ph],
                        device_id=(w, t), device_id_type=MESH,
                    ).start()

                return inner

            lax.fori_loop(0, N_TRANS, go, 0, unroll=4)
            return carry

        lax.fori_loop(0, N_WELD, row, 0)
        dst[me] = src[me]

    def all_to_all_wait(src, dst, ph):
        part = dst.at[pl.ds(0, OWN - 1)]
        pltpu.make_async_copy(part, part, asem_r.at[ph]).wait()
        part = src.at[pl.ds(0, OWN - 1)]
        pltpu.make_async_copy(part, part, asem_s.at[ph]).wait()

    def partner_copies(src, dst, ph):
        out = []
        for bit in range(2):
            step = 1 << bit
            other = weld + step - 2 * step * ((weld // step) % 2)
            out.append(
                pltpu.make_async_remote_copy(
                    src, dst.at[bit], hsem_s.at[ph, bit], hsem_r.at[ph, bit],
                    device_id=(other, trans), device_id_type=MESH,
                )
            )
        return out

    my_bit = bit_ref[0]

    def picked(ref):
        return jnp.where(my_bit == 0, ref[0].astype(f32), ref[1].astype(f32))

    def scatter_pair(q, s0, s1):
        t0, t1 = s0 * m0_ref[q], s1 * m1_ref[q]
        lhs = [
            jnp.concatenate([jnp.where(lo, t, 0.0), jnp.where(lo, 0.0, t)], 0).astype(bf16)
            for t in (t0, t1)
        ]
        w_pair = w_ref[pl.ds(2 * q, 2)].reshape(128, 256)
        return dot(lhs[0], w_pair[:, 0:128]) + dot(lhs[1], w_pair[:, 128:256])

    def scatter_put(q, res):
        pt_ref[pl.ds(pl.multiple_of(q * 16, 16), 16), :] = res

    def build_pair(q):
        lanes = pl.ds(pl.multiple_of(q * 128, 128), 128)

        def row(r):
            return jnp.broadcast_to(st_ref[r : r + 1, lanes], (8, 128))

        xy, yz, xz = row(7), row(8), row(9)
        s0 = jnp.where(row8 < 4, st_ref[0:8, lanes], jnp.where(row8 == 4, 1.0, xz))
        s0 = jnp.where(row8 == 5, row(4), jnp.where(row8 == 6, xy, s0))
        s1 = jnp.where(row8 == 0, xy, jnp.where(row8 == 1, row(5), yz))
        s1 = jnp.where(row8 == 5, xz, jnp.where(row8 == 7, row(6), s1))
        s1 = jnp.where(gap, 0.0, s1)
        many = jnp.where(lo, cnt_ref[2 * q], cnt_ref[2 * q + 1])
        live = lane64 < many
        mass8 = jnp.where(live, jnp.broadcast_to(mass_ref[0:1, lanes], (8, 128)), 0.0)
        stiff8 = jnp.where(live, 0.25 * jnp.broadcast_to(stiff_ref[0:1, lanes], (8, 128)), 0.0)
        return (
            s0,
            s1,
            jnp.where(row8 < 5, mass8, -0.25 * mass8),
            -0.25 * mass8,
            jnp.where(row8 < 5, 0.0, stiff8),
            jnp.where(gap, 0.0, stiff8),
        )

    tile_refs = (s0_ref, s1_ref, m0_ref, m1_ref, f0_ref, f1_ref)

    def build_group(g, carry):
        group = [4 * g + p for p in range(4)]
        built = [build_pair(q) for q in group]
        for q, tiles in zip(group, built):
            for ref, tile in zip(tile_refs, tiles):
                ref[q] = tile
        return carry

    def scatter_group(g, carry):
        group = [GROUP * g + p for p in range(GROUP)]
        sums = [scatter_pair(q, s0_ref[q], s1_ref[q]) for q in group]
        for q, res in zip(group, sums):
            scatter_put(q, res)
        return carry

    hi = jnp.logical_not(lo)

    def rows_in(*which):
        hit = row8 == which[0]
        for w in which[1:]:
            hit = jnp.logical_or(hit, row8 == w)
        return hit

    def mask(*terms):
        total = jnp.zeros((8, 128), f32)
        for value, which, lanes in terms:
            total = total + jnp.where(jnp.logical_and(rows_in(*which), lanes), value, 0.0)
        return total

    f0h0 = [
        mask((1.0, (0,), lo), (1.0, (6,), hi)),
        mask((1.0, (2,), lo)),
        mask((1.0, (1,), lo), (2.0, (5,), hi)),
        mask((1.0, (3,), lo), (1.0, (7,), hi)),
    ]
    f0h1 = [mask((1.0, (6,), lo)), None, mask((1.0, (7,), hi)), None]
    f1h0 = [
        mask((1.0, (0,), hi)),
        None,
        mask((1.0, (3,), hi)),
        mask((1.0, (5,), hi)),
    ]
    f1h1 = [
        mask((1.0, (0,), lo), (1.0, (2, 6), hi)),
        mask((1.0, (2, 6), lo)),
        mask((2.0, (1,), lo), (1.0, (3,), lo), (1.0, (5,), hi)),
        mask((1.0, (3,), hi), (2.0, (7,), hi)),
    ]

    def combine(masks, vals):
        total = None
        for m, v in zip(masks, vals):
            if m is not None:
                term = m * v
                total = term if total is None else total + term
        return total

    def gather_pair(q):
        left, right = [], []
        for b in range(2):
            vals = [
                jnp.broadcast_to(fbx_ref[2 * q + b, g : g + 1, :], (8, 128)) for g in range(4)
            ]
            left += [combine(f0h0, vals), combine(f1h0, vals)]
            right += [combine(f0h1, vals), combine(f1h1, vals)]
        lhs = jnp.concatenate(
            [jnp.concatenate(left, 0).astype(bf16), jnp.concatenate(right, 0).astype(bf16)], 1
        )
        res = dot_nt(lhs, w_ref[pl.ds(2 * q, 2)].reshape(128, 256))
        o0 = jnp.where(lo, res[0:8], res[16:24])
        o1 = jnp.where(lo, res[8:16], res[24:32])
        trace = jnp.broadcast_to(o1[3:4], (8, 128))
        s0, s1 = s0_ref[q], s1_ref[q]
        fresh = jnp.logical_and(m0_ref[q] > 0.0, row8 < 4)
        s0 = jnp.where(fresh, o0, s0 + f0_ref[q] * jnp.where(row8 == 5, o0 + trace, o0))
        s1 = s1 + f1_ref[q] * jnp.where(
            jnp.logical_or(row8 == 1, row8 == 7), o1 + trace, o1
        )
        return s0, s1

    def middle_group(g, carry):
        group = [GROUP * g + p for p in range(GROUP)]
        state = [gather_pair(q) for q in group]
        sums = [scatter_pair(q, *st) for q, st in zip(group, state)]
        for q, (s0, s1), res in zip(group, state, sums):
            s0_ref[q] = s0
            s1_ref[q] = s1
            scatter_put(q, res)
        return carry

    def natural(s0, s1):
        top = jnp.where(row8 < 4, s0, pltpu.roll(s0, 7, 0))
        top = jnp.where(row8 == 5, pltpu.roll(s1, 4, 0), top)
        top = jnp.where(row8 == 6, pltpu.roll(s1, 7, 0), top)
        top = jnp.where(row8 == 7, pltpu.roll(s0, 1, 0), top)
        low = jnp.where(row8 == 0, pltpu.roll(s1, 6, 0), pltpu.roll(s0, 2, 0))
        return top, low

    def last_tiles(first, dst):
        def body(g, carry):
            group = [GROUP * g + p for p in range(GROUP)]
            state = [natural(*gather_pair(q)) for q in group]
            for q, (top, low) in zip(group, state):
                lanes = pl.ds(pl.multiple_of((q - first) * 128, 128), 128)
                dst[0:8, lanes] = top
                dst[8:10, lanes] = low[0:2]
            return carry

        return body

    last_group = last_tiles(0, out_ref)
    last_extra = last_tiles(PAIRS, xs)

    pt_ref[pl.ds(ALLP * 16, (EXT // 2 - ALLP) * 16), :] = jnp.zeros(
        ((EXT // 2 - ALLP) * 16, 128), f32
    )

    def first_chunk(c, carry):
        chunk_copy(c).wait()
        return lax.fori_loop(
            0, CHP // GROUP, lambda i, got: scatter_group(c * (CHP // GROUP) + i, got), carry
        )

    lax.fori_loop(0, PAIRS // 4, build_group, 0)
    lax.fori_loop(0, EARLY, first_chunk, 0)
    for c in range(EARLY, CHUNKS):
        chunk_copy(c).wait()

    def take_extra(i, carry):
        blk_ids = [swap_ref[0, 2 * i + b] for b in range(2)]
        for b in range(2):
            w_ref[PB + 2 * i + b] = w_ref[blk_ids[b]]
        for ref in tile_refs:
            vals = []
            for b in range(2):
                v = ref[lax.div(blk_ids[b], 2)]
                vals.append(jnp.where(lax.rem(blk_ids[b], 2) == b, v, pltpu.roll(v, 64, 1)))
            ref[PAIRS + i] = jnp.where(lo, vals[0], vals[1])
        return carry

    lax.fori_loop(0, XPAIRS, take_extra, 0, unroll=4)
    lax.fori_loop(NAT, ALLP // GROUP, scatter_group, 0)

    def channels(first, count, groups):
        lo_c = iota((count, 128), 1) < 64
        v = [pt_ref[pl.ds(first * 8 + c, count, stride=8), :] for c in range(8)]
        parts = [
            jnp.where(lo_c, v[0], v[6]) + pltpu.roll(jnp.where(lo_c, v[1], v[5]), 64, 1),
            jnp.where(lo_c, v[2], 0.0) + pltpu.roll(jnp.where(lo_c, v[3], v[7]), 64, 1),
        ]
        if groups > 2:
            parts.append(v[4])
        return parts

    tgt = tgt_ref[...].astype(f32)
    own_r = jnp.floor(tgt * (1.0 / NBD))
    node_r = tgt - NBD * own_r + 1.0

    sw_row = iota((SWP, 128), 0)
    sw_col = jnp.full((SWP, 128), -1, jnp.int32)
    for s in range(SW):
        sw_col = jnp.where(sw_row == s, swap_ref[0, s], sw_col)
    flags, own_h, node_h = [], 0.0, 0.0
    for j in range(3):
        hits = (sw_col == iota((SWP, 128), 1) + 128 * j).astype(f32)
        flags.append(jnp.sum(hits, 0, keepdims=True))
        own_h = own_h + jnp.sum(hits * own_r[j : j + 1], 1, keepdims=True)
        node_h = node_h + jnp.sum(hits * node_r[j : j + 1], 1, keepdims=True)
    own_h = jnp.where(sw_row < SW, jnp.broadcast_to(own_h, (SWP, 128)), -1.0)
    node_h = jnp.broadcast_to(node_h, (SWP, 128))

    parts = channels(PB, SWP, 3)
    lo_s = iota((SWP, 128), 1) < 64
    hs1[...] = jnp.concatenate(
        [parts[0], parts[1], jnp.where(lo_s, parts[2], node_h), own_h], 1
    ).astype(bf16)

    pl.semaphore_wait(bar, OWN - 1)
    hand1 = partner_copies(hs1, hr1, 0)
    for c in hand1:
        c.start()
    lax.fori_loop(EARLY * CHP // GROUP, NAT, scatter_group, 0)

    own_cols = []
    for j in range(3):
        lanes = slice(j * 128, j * 128 + 128)
        own_j = jnp.where(flags[j] > 0.0, -1.0, own_r[j : j + 1])
        own_b = jnp.broadcast_to(own_j, (128, 128))
        kr_ref[:, lanes] = own_b
        own_cols.append(own_b.T)
        node_c = jnp.broadcast_to(node_r[j : j + 1], (128, 128)).T
        parts = channels(j * 128, 128, 3)
        lo_b = iota((128, 128), 1) < 64
        pb_ref[lanes, :] = jnp.concatenate(
            [parts[0], parts[1], jnp.where(lo_b, parts[2], node_c)], 1
        ).astype(bf16)
    pb_ref[PB:EXT, :] = jnp.zeros((EXT - PB, 384), bf16)

    for c in hand1:
        c.wait()
    got = picked(hr1)
    pb_ref[PB : PB + SWP, :] = got[:, 0:384].astype(bf16)
    own_cols.append(jnp.concatenate([got[:, 384:512], jnp.full((96, 128), -1.0, f32)], 0))
    kr_ref[:, PB:EXT] = own_cols[3].T

    before = iota((128, 128), 1) < iota((128, 128), 0)
    for i in range(4):
        count = jnp.zeros((128, 128), f32)
        for j in range(i + 1):
            same = own_cols[i] == kr_ref[:, j * 128 : j * 128 + 128]
            if j == i:
                same = jnp.logical_and(same, before)
            count = count + jnp.where(same, 1.0, 0.0)
        rank = jnp.broadcast_to(jnp.sum(count, 1, keepdims=True), (128, 128))
        key = jnp.where(own_cols[i] >= 0.0, own_cols[i] * SLOTS + rank, -1.0)
        kc_ref[i * 128 : i * 128 + 128, :] = key
    for i in range(4):
        kr_ref[:, i * 128 : i * 128 + 128] = kc_ref[i * 128 : i * 128 + 128, :].T

    def send_rows(c, groups):
        r = iota((128, EXT), 0) + c * 128
        row_key = ((r // 8) * SLOTS + r % SLOTS).astype(f32)
        pick = jnp.where(row_key == kr_ref[...], 1.0, 0.0).astype(bf16)
        res = dot(pick, pb_ref[:, 0 : groups * 128])
        first_half = (iota((128, 128), 0) % 8) < SLOTS
        main = jnp.where(first_half, res[:, 0:128], res[:, 128:256])
        return main.reshape(16, 8, 128), res[:, 256:]

    def fill1(c):
        main, extra = send_rows(c, 3)
        owners = pl.ds(pl.multiple_of(c * 16, 16), 16)
        send1[owners] = jnp.concatenate([main, extra.reshape(16, 8, 128)], 1).astype(bf16)

    all_to_all(fill1, send1, recv1, 0)

    key_lane = iota((EXT, 128), 1)
    for c in range(8):
        lane_key = (((key_lane + c * 128) // 8) * SLOTS + key_lane % SLOTS).astype(f32)
        sd_ref[:, c * 128 : c * 128 + 128] = jnp.where(
            kc_ref[...] == lane_key, 1.0, 0.0
        ).astype(bf16)

    all_to_all_wait(send1, recv1, 0)

    half0 = (iota((128, 128), 0) % 8) < SLOTS
    node_lane = (iota((128, 128), 1) - (NBD - 1)).astype(f32)

    def grid_sum1(c):
        blocks = recv1[c * 16 : c * 16 + 16].astype(f32)
        main = blocks[:, 0:8].reshape(128, 128)
        extra = blocks[:, 8:16].reshape(128, 128)
        hit = jnp.where(
            jnp.logical_and(extra == node_lane, node_lane > 0.0), 1.0, 0.0
        )
        at_ref[c * 128 : c * 128 + 128, :] = hit.astype(bf16)
        hit_t = hit.T.astype(bf16)
        a_ref[:, c * 128 : c * 128 + 128] = hit_t
        rhs = jnp.concatenate(
            [
                jnp.where(half0, main, 0.0),
                jnp.where(half0, 0.0, main),
                jnp.where(half0, extra, 0.0),
            ],
            1,
        ).astype(bf16)
        return dot(hit_t, rhs)

    def grid_sum2(c):
        main = recv2[c * 16 : c * 16 + 16].astype(f32).reshape(128, 128)
        rhs = jnp.concatenate(
            [jnp.where(half0, main, 0.0), jnp.where(half0, 0.0, main)], 1
        ).astype(bf16)
        return dot(a_ref[:, c * 128 : c * 128 + 128], rhs)

    lane_n = iota((NBD, 128), 1)
    keep0 = (lane_n % 64) >= 8
    keep1 = jnp.logical_or(lane_n >= 64, lane_n >= 8)

    def grid_fields(total, msafe):
        vel = jnp.where(keep0, total[NBD:, 0:128] / msafe, 0.0)
        rest = jnp.where(keep1, total[NBD:, 128:256] / msafe, 0.0)
        return jnp.concatenate([vel, rest], 1).astype(bf16)

    def answer(fields, ph):
        rhs = jnp.concatenate([jnp.zeros((NBD, 256), bf16), fields], 0)

        def fill(c):
            rows = pl.ds(pl.multiple_of(c * 128, 128), 128)
            res = dot(at_ref[rows, :], rhs)
            main = jnp.where(half0, res[:, 0:128], res[:, 128:256])
            owners = pl.ds(pl.multiple_of(c * 16, 16), 16)
            ans_s[ph, owners] = main.reshape(16, 8, 128).astype(bf16)

        all_to_all(fill, ans_s.at[ph], ans_r.at[ph], 1 + 2 * ph)

    def put_fields(first, count, fields):
        flat = fbx_ref.reshape(EXT * 8, 128)
        a, b = fields[0:count, 0:128], fields[0:count, 128:256]
        for g, val in enumerate((a, b, pltpu.roll(a, 64, 1), pltpu.roll(b, 64, 1))):
            flat[pl.ds(first * 8 + g, count, stride=8), :] = val

    def spread(src, ph):
        total = jnp.zeros((EXT, 256), f32)
        for c in range(4):
            main = src[c * 32 : c * 32 + 32].astype(f32).reshape(256, 128)
            first_half = (iota((256, 128), 0) % 8) < SLOTS
            rhs = jnp.concatenate(
                [jnp.where(first_half, main, 0.0), jnp.where(first_half, 0.0, main)], 1
            ).astype(bf16)
            total = total + dot(sd_ref[:, c * 256 : c * 256 + 256], rhs)
        fs[ph] = total[PB : PB + SWP].astype(bf16)
        copies = partner_copies(fs.at[ph], fr.at[ph], 1 + ph)
        for c in copies:
            c.start()
        put_fields(0, PB, total)
        return copies

    def spread_end(copies, ph):
        for c in copies:
            c.wait()
        got = picked(fr.at[ph])
        put_fields(PB, SWP, got)

    total = grid_sum1(0)
    for c in range(1, 8):
        total = total + grid_sum1(c)
    mass_n = total[NBD:, 256:384]
    msafe = jnp.maximum(jnp.where(lane_n < 64, mass_n, pltpu.roll(mass_n, 64, 1)), 0.25)
    ms_ref[...] = msafe
    answer(grid_fields(total, msafe), 0)
    all_to_all_wait(ans_s.at[0], ans_r.at[0], 1)

    copies = spread(ans_r.at[0], 0)
    lax.fori_loop(0, NAT // 2, middle_group, 0)
    spread_end(copies, 0)
    lax.fori_loop(NAT, ALLP // GROUP, middle_group, 0)
    hs2[...] = jnp.concatenate(channels(PB, SWP, 2), 1).astype(bf16)
    hand2 = partner_copies(hs2, hr2, 3)
    for c in hand2:
        c.start()
    lax.fori_loop(NAT // 2, NAT, middle_group, 0)
    for j in range(3):
        pb_ref[j * 128 : j * 128 + 128, 0:256] = jnp.concatenate(
            channels(j * 128, 128, 2), 1
        ).astype(bf16)
    for c in hand2:
        c.wait()
    pb_ref[PB : PB + SWP, 0:256] = picked(hr2).astype(bf16)

    def fill2(c):
        main, _ = send_rows(c, 2)
        send2[pl.ds(pl.multiple_of(c * 16, 16), 16)] = main.astype(bf16)

    all_to_all(fill2, send2, recv2, 2)
    all_to_all_wait(send2, recv2, 2)
    total = grid_sum2(0)
    for c in range(1, 8):
        total = total + grid_sum2(c)
    fields = grid_fields(total, ms_ref[...])
    field_ref[...] = fields
    answer(fields, 1)
    all_to_all_wait(ans_s.at[1], ans_r.at[1], 3)

    copies = spread(ans_r.at[1], 1)
    lax.fori_loop(0, NAT // 2, last_group, 0)
    spread_end(copies, 1)
    lax.fori_loop(NAT, ALLP // GROUP, last_extra, 0)
    hand3 = partner_copies(xs, xr, 4)
    for c in hand3:
        c.start()
    lax.fori_loop(NAT // 2, NAT, last_group, 0)
    for c in hand3:
        c.wait()
    xout_ref[...] = picked(xr)


def weld_call(weights, state, mass, stiff, targets, counts, bit, swap):
    vmem = pl.BlockSpec(memory_space=pltpu.VMEM)
    smem = pl.BlockSpec(memory_space=pltpu.SMEM)
    dma = pltpu.SemaphoreType.DMA
    return pl.pallas_call(
        weld_kernel,
        out_shape=(
            jax.ShapeDtypeStruct((10, PB * BS), f32),
            jax.ShapeDtypeStruct((NBD, 4 * BS), bf16),
            jax.ShapeDtypeStruct((16, XPAIRS * 128), f32),
        ),
        in_specs=[pl.BlockSpec(memory_space=pl.ANY), vmem, vmem, vmem, vmem, smem, smem, smem],
        out_specs=(vmem, vmem, vmem),
        scratch_shapes=[
            pltpu.VMEM((2 * ALLP, BS, 4 * BS), bf16),
            pltpu.VMEM((ALLP, 8, 128), f32),
            pltpu.VMEM((ALLP, 8, 128), f32),
            pltpu.VMEM((ALLP, 8, 128), f32),
            pltpu.VMEM((ALLP, 8, 128), f32),
            pltpu.VMEM((ALLP, 8, 128), f32),
            pltpu.VMEM((ALLP, 8, 128), f32),
            pltpu.VMEM((EXT * 8, 128), f32),
            pltpu.VMEM((EXT, 384), bf16),
            pltpu.VMEM((EXT, 8, 128), f32),
            pltpu.VMEM((EXT, 128), f32),
            pltpu.VMEM((128, EXT), f32),
            pltpu.VMEM((EXT, ROWS), bf16),
            pltpu.VMEM((ROWS, 128), bf16),
            pltpu.VMEM((128, ROWS), bf16),
            pltpu.VMEM((NBD, 128), f32),
            pltpu.VMEM((OWN, 16, 128), bf16),
            pltpu.VMEM((OWN, 16, 128), bf16),
            pltpu.VMEM((OWN, 8, 128), bf16),
            pltpu.VMEM((OWN, 8, 128), bf16),
            pltpu.VMEM((2, OWN, 8, 128), bf16),
            pltpu.VMEM((2, OWN, 8, 128), bf16),
            pltpu.VMEM((SWP, 512), bf16),
            pltpu.VMEM((2, SWP, 512), bf16),
            pltpu.VMEM((SWP, 256), bf16),
            pltpu.VMEM((2, SWP, 256), bf16),
            pltpu.VMEM((2, SWP, 256), bf16),
            pltpu.VMEM((2, 2, SWP, 256), bf16),
            pltpu.VMEM((16, XPAIRS * 128), f32),
            pltpu.VMEM((2, 16, XPAIRS * 128), f32),
            dma((CHUNKS,)),
            dma((4,)),
            dma((4,)),
            dma((5, 2)),
            dma((5, 2)),
        ],
        compiler_params=pltpu.CompilerParams(
            collective_id=0, has_side_effects=True, vmem_limit_bytes=56 * 1024 * 1024
        ),
    )(weights, state, mass, stiff, targets, counts, bit, swap)


def place_kernel(own_hbm, got_hbm, fields_hbm, swap_ref, out_ref, fields_out, got_ref, sem):
    copies = [
        pltpu.make_async_copy(src, dst, sem.at[i])
        for i, (src, dst) in enumerate(
            ((own_hbm, out_ref), (got_hbm, got_ref), (fields_hbm, fields_out))
        )
    ]
    for c in copies:
        c.start()
    lane = iota((8, 128), 1)
    for c in copies:
        c.wait()
    for s in range(SW):
        blk_id = swap_ref[0, s]
        src = slice((s // 2) * 128, (s // 2) * 128 + 128)
        dst = pl.ds(pl.multiple_of((blk_id // 2) * 128, 128), 128)
        same = (s % 2) == (blk_id % 2)
        mine = (lane >= 64) == (blk_id % 2 == 1)
        top, low = got_ref[0:8, src], got_ref[8:16, src]
        top = jnp.where(same, top, pltpu.roll(top, 64, 1))
        low = jnp.where(same, low, pltpu.roll(low, 64, 1))
        out_ref[0:8, dst] = jnp.where(mine, top, out_ref[0:8, dst])
        out_ref[8:10, dst] = jnp.where(mine[0:2], low[0:2], out_ref[8:10, dst])


def place_call(own, got, fields, swap):
    vmem = pl.BlockSpec(memory_space=pltpu.VMEM)
    hbm = pl.BlockSpec(memory_space=pl.ANY)
    return pl.pallas_call(
        place_kernel,
        out_shape=(
            jax.ShapeDtypeStruct((10, PB * BS), f32),
            jax.ShapeDtypeStruct((NBD, 4 * BS), bf16),
        ),
        in_specs=[hbm, hbm, hbm, pl.BlockSpec(memory_space=pltpu.SMEM)],
        out_specs=(vmem, hbm),
        scratch_shapes=[
            pltpu.VMEM((16, XPAIRS * 128), f32),
            pltpu.SemaphoreType.DMA((3,)),
        ],
        compiler_params=pltpu.CompilerParams(vmem_limit_bytes=56 * 1024 * 1024),
    )(own, got, fields, swap)


def shards(weights, particle_state, mass, stiffness, targets, counts, partner_bit, swap_list):
    own, fields, got = weld_call(
        weights,
        particle_state,
        mass.reshape(1, PB * BS),
        stiffness.reshape(1, PB * BS),
        targets.reshape(3, 128),
        counts,
        partner_bit,
        swap_list,
    )
    return place_call(own, got, fields, swap_list)


def solution(mesh):
    both = ("weld", "trans")
    in_specs = (
        P(both, None, None),
        P(None, both),
        P(both),
        P(both),
        P(both),
        P(both),
        P(both),
        P(both, None),
    )
    out_specs = (P(None, both), P(both, None))
    return jax.shard_map(shards, mesh=mesh, in_specs=in_specs, out_specs=out_specs, check_vma=False)
```

```python
import functools

import jax
import jax.numpy as jnp
from jax import lax
from jax.experimental import pallas as pl
from jax.experimental.pallas import tpu as pltpu
from jax.sharding import PartitionSpec as P

BS = 64
NBD = 64
PB = 384
SW = 24
N_WELD = 8
N_TRANS = 16
OWN = 128
SLOTS = 4
PAIRS = PB // 2
XPAIRS = SW // 2
ALLP = PAIRS + XPAIRS
ROWS = OWN * 2 * SLOTS
EXT = 512
SWP = 32
GROUP = 12
CHP = 12
CHUNKS = PAIRS // CHP
NAT = PAIRS // GROUP
EARLY = CHUNKS * 2 // 3

f32 = jnp.float32
bf16 = jnp.bfloat16
MESH = pl.DeviceIdType.MESH


def iota(shape, dim):
    return lax.broadcasted_iota(jnp.int32, shape, dim)


def coords(dev):
    return (dev // N_TRANS, dev % N_TRANS)


def dot(lhs, rhs):
    return lax.dot_general(lhs, rhs, (((1,), (0,)), ((), ())), preferred_element_type=f32)


def dot_nt(lhs, rhs):
    return lax.dot_general(lhs, rhs, (((1,), (1,)), ((), ())), preferred_element_type=f32)


def weld_kernel(
    w_hbm, st_ref, mass_ref, stiff_ref, tgt_ref, cnt_ref, bit_ref, swap_ref,
    out_ref, field_ref, xout_ref,
    w_ref, s0_ref, s1_ref, m0_ref, m1_ref, f0_ref, f1_ref, pt_ref, pb_ref, fbx_ref, kc_ref, kr_ref,
    sd_ref, pick_ref, at_ref, a_ref, ms_ref,
    send1, recv1, send2, recv2, ans_s, ans_r,
    hs1, hr1, hs2, hr2, fs, fr, xs, xr,
    wsem, asem_s, asem_r, hsem_s, hsem_r,
):
    weld = lax.axis_index("weld")
    trans = lax.axis_index("trans")
    me = weld * N_TRANS + trans
    bar = pltpu.get_barrier_semaphore()

    def chunk_copy(c):
        part = pl.ds(c * CHP * 2, CHP * 2)
        return pltpu.make_async_copy(w_hbm.at[part], w_ref.at[part], wsem.at[c])

    for c in range(CHUNKS):
        chunk_copy(c).start()

    def greet(j, carry):
        pl.semaphore_signal(
            bar, inc=1, device_id=coords(lax.rem(me + j, OWN)), device_id_type=MESH
        )
        return carry

    lax.fori_loop(1, OWN, greet, 0)

    row8 = iota((8, 128), 0)
    lane8 = iota((8, 128), 1)
    lo = lane8 < 64
    lane64 = lane8 % 64
    gap = jnp.logical_or(row8 == 3, row8 == 4)

    def all_to_all(fill, src, dst, ph):
        def row(i, carry):
            w = lax.rem(weld + N_WELD // 2 + i, N_WELD)
            fill(w)

            def go(j, inner):
                t = lax.rem(trans + N_TRANS // 2 + j, N_TRANS)
                dev = w * N_TRANS + t

                @pl.when(dev != me)
                def _():
                    pltpu.make_async_remote_copy(
                        src.at[dev], dst.at[me], asem_s.at[ph], asem_r.at[ph],
                        device_id=(w, t), device_id_type=MESH,
                    ).start()

                return inner

            lax.fori_loop(0, N_TRANS, go, 0, unroll=8)
            return carry

        lax.fori_loop(0, N_WELD, row, 0)
        dst[me] = src[me]

    def all_to_all_wait(src, dst, ph):
        part = dst.at[pl.ds(0, OWN - 1)]
        pltpu.make_async_copy(part, part, asem_r.at[ph]).wait()
        part = src.at[pl.ds(0, OWN - 1)]
        pltpu.make_async_copy(part, part, asem_s.at[ph]).wait()

    def partner_copies(src, dst, ph):
        out = []
        for bit in range(2):
            step = 1 << bit
            other = weld + step - 2 * step * ((weld // step) % 2)
            out.append(
                pltpu.make_async_remote_copy(
                    src, dst.at[bit], hsem_s.at[ph, bit], hsem_r.at[ph, bit],
                    device_id=(other, trans), device_id_type=MESH,
                )
            )
        return out

    my_bit = bit_ref[0]

    def picked(ref):
        return jnp.where(my_bit == 0, ref[0].astype(f32), ref[1].astype(f32))

    def scatter_pair(q, s0, s1):
        t0, t1 = s0 * m0_ref[q], s1 * m1_ref[q]
        lhs = [
            jnp.concatenate([jnp.where(lo, t, 0.0), jnp.where(lo, 0.0, t)], 0).astype(bf16)
            for t in (t0, t1)
        ]
        w_pair = w_ref[pl.ds(2 * q, 2)].reshape(128, 256)
        return dot(lhs[0], w_pair[:, 0:128]) + dot(lhs[1], w_pair[:, 128:256])

    def scatter_put(q, res):
        pt_ref[pl.ds(pl.multiple_of(q * 16, 16), 16), :] = res

    def build_pair(q):
        lanes = pl.ds(pl.multiple_of(q * 128, 128), 128)

        def row(r):
            return jnp.broadcast_to(st_ref[r : r + 1, lanes], (8, 128))

        xy, yz, xz = row(7), row(8), row(9)
        s0 = jnp.where(row8 < 4, st_ref[0:8, lanes], jnp.where(row8 == 4, 1.0, xz))
        s0 = jnp.where(row8 == 5, row(4), jnp.where(row8 == 6, xy, s0))
        s1 = jnp.where(row8 == 0, xy, jnp.where(row8 == 1, row(5), yz))
        s1 = jnp.where(row8 == 5, xz, jnp.where(row8 == 7, row(6), s1))
        s1 = jnp.where(gap, 0.0, s1)
        many = jnp.where(lo, cnt_ref[2 * q], cnt_ref[2 * q + 1])
        live = lane64 < many
        mass8 = jnp.where(live, jnp.broadcast_to(mass_ref[0:1, lanes], (8, 128)), 0.0)
        stiff8 = jnp.where(live, 0.25 * jnp.broadcast_to(stiff_ref[0:1, lanes], (8, 128)), 0.0)
        return (
            s0,
            s1,
            jnp.where(row8 < 5, mass8, -0.25 * mass8),
            -0.25 * mass8,
            jnp.where(row8 < 5, 0.0, stiff8),
            jnp.where(gap, 0.0, stiff8),
        )

    tile_refs = (s0_ref, s1_ref, m0_ref, m1_ref, f0_ref, f1_ref)

    def build_group(g, carry):
        group = [4 * g + p for p in range(4)]
        built = [build_pair(q) for q in group]
        for q, tiles in zip(group, built):
            for ref, tile in zip(tile_refs, tiles):
                ref[q] = tile
        return carry

    def scatter_group(g, carry):
        group = [GROUP * g + p for p in range(GROUP)]
        sums = [scatter_pair(q, s0_ref[q], s1_ref[q]) for q in group]
        for q, res in zip(group, sums):
            scatter_put(q, res)
        return carry

    hi = jnp.logical_not(lo)

    def rows_in(*which):
        hit = row8 == which[0]
        for w in which[1:]:
            hit = jnp.logical_or(hit, row8 == w)
        return hit

    def mask(*terms):
        total = jnp.zeros((8, 128), f32)
        for value, which, lanes in terms:
            total = total + jnp.where(jnp.logical_and(rows_in(*which), lanes), value, 0.0)
        return total

    f0h0 = [
        mask((1.0, (0,), lo), (1.0, (6,), hi)),
        mask((1.0, (2,), lo)),
        mask((1.0, (1,), lo), (2.0, (5,), hi)),
        mask((1.0, (3,), lo), (1.0, (7,), hi)),
    ]
    f0h1 = [mask((1.0, (6,), lo)), None, mask((1.0, (7,), hi)), None]
    f1h0 = [
        mask((1.0, (0,), hi)),
        None,
        mask((1.0, (3,), hi)),
        mask((1.0, (5,), hi)),
    ]
    f1h1 = [
        mask((1.0, (0,), lo), (1.0, (2, 6), hi)),
        mask((1.0, (2, 6), lo)),
        mask((2.0, (1,), lo), (1.0, (3,), lo), (1.0, (5,), hi)),
        mask((1.0, (3,), hi), (2.0, (7,), hi)),
    ]

    def combine(masks, vals):
        total = None
        for m, v in zip(masks, vals):
            if m is not None:
                term = m * v
                total = term if total is None else total + term
        return total

    def gather_pair(q):
        left, right = [], []
        for b in range(2):
            vals = [
                jnp.broadcast_to(fbx_ref[2 * q + b, g : g + 1, :], (8, 128)) for g in range(4)
            ]
            left += [combine(f0h0, vals), combine(f1h0, vals)]
            right += [combine(f0h1, vals), combine(f1h1, vals)]
        lhs = jnp.concatenate(
            [jnp.concatenate(left, 0).astype(bf16), jnp.concatenate(right, 0).astype(bf16)], 1
        )
        res = dot_nt(lhs, w_ref[pl.ds(2 * q, 2)].reshape(128, 256))
        o0 = jnp.where(lo, res[0:8], res[16:24])
        o1 = jnp.where(lo, res[8:16], res[24:32])
        trace = jnp.broadcast_to(o1[3:4], (8, 128))
        s0, s1 = s0_ref[q], s1_ref[q]
        fresh = jnp.logical_and(m0_ref[q] > 0.0, row8 < 4)
        s0 = jnp.where(fresh, o0, s0 + f0_ref[q] * jnp.where(row8 == 5, o0 + trace, o0))
        s1 = s1 + f1_ref[q] * jnp.where(
            jnp.logical_or(row8 == 1, row8 == 7), o1 + trace, o1
        )
        return s0, s1

    def middle_group(g, carry):
        group = [GROUP * g + p for p in range(GROUP)]
        state = [gather_pair(q) for q in group]
        sums = [scatter_pair(q, *st) for q, st in zip(group, state)]
        for q, (s0, s1), res in zip(group, state, sums):
            s0_ref[q] = s0
            s1_ref[q] = s1
            scatter_put(q, res)
        return carry

    def natural(s0, s1):
        top = jnp.where(row8 < 4, s0, pltpu.roll(s0, 7, 0))
        top = jnp.where(row8 == 5, pltpu.roll(s1, 4, 0), top)
        top = jnp.where(row8 == 6, pltpu.roll(s1, 7, 0), top)
        top = jnp.where(row8 == 7, pltpu.roll(s0, 1, 0), top)
        low = jnp.where(row8 == 0, pltpu.roll(s1, 6, 0), pltpu.roll(s0, 2, 0))
        return top, low

    def last_tiles(first, dst):
        def body(g, carry):
            group = [GROUP * g + p for p in range(GROUP)]
            state = [natural(*gather_pair(q)) for q in group]
            for q, (top, low) in zip(group, state):
                lanes = pl.ds(pl.multiple_of((q - first) * 128, 128), 128)
                dst[0:8, lanes] = top
                dst[8:10, lanes] = low[0:2]
            return carry

        return body

    last_group = last_tiles(0, out_ref)
    last_extra = last_tiles(PAIRS, xs)

    pt_ref[pl.ds(ALLP * 16, (EXT // 2 - ALLP) * 16), :] = jnp.zeros(
        ((EXT // 2 - ALLP) * 16, 128), f32
    )

    def first_chunk(c, carry):
        chunk_copy(c).wait()
        return lax.fori_loop(
            0, CHP // GROUP, lambda i, got: scatter_group(c * (CHP // GROUP) + i, got), carry
        )

    lax.fori_loop(0, PAIRS // 4, build_group, 0)
    lax.fori_loop(0, EARLY, first_chunk, 0)
    for c in range(EARLY, CHUNKS):
        chunk_copy(c).wait()

    def take_extra(i, carry):
        blk_ids = [swap_ref[0, 2 * i + b] for b in range(2)]
        for b in range(2):
            w_ref[PB + 2 * i + b] = w_ref[blk_ids[b]]
        for ref in tile_refs:
            vals = []
            for b in range(2):
                v = ref[lax.div(blk_ids[b], 2)]
                vals.append(jnp.where(lax.rem(blk_ids[b], 2) == b, v, pltpu.roll(v, 64, 1)))
            ref[PAIRS + i] = jnp.where(lo, vals[0], vals[1])
        return carry

    lax.fori_loop(0, XPAIRS, take_extra, 0, unroll=4)
    lax.fori_loop(NAT, ALLP // GROUP, scatter_group, 0)

    def channels(first, count, groups):
        lo_c = iota((count, 128), 1) < 64
        v = [pt_ref[pl.ds(first * 8 + c, count, stride=8), :] for c in range(8)]
        parts = [
            jnp.where(lo_c, v[0], v[6]) + pltpu.roll(jnp.where(lo_c, v[1], v[5]), 64, 1),
            jnp.where(lo_c, v[2], 0.0) + pltpu.roll(jnp.where(lo_c, v[3], v[7]), 64, 1),
        ]
        if groups > 2:
            parts.append(v[4])
        return parts

    tgt = tgt_ref[...].astype(f32)
    own_r = jnp.floor(tgt * (1.0 / NBD))
    node_r = tgt - NBD * own_r + 1.0

    sw_row = iota((SWP, 128), 0)
    sw_col = jnp.full((SWP, 128), -1, jnp.int32)
    for s in range(SW):
        sw_col = jnp.where(sw_row == s, swap_ref[0, s], sw_col)
    flags, own_h, node_h = [], 0.0, 0.0
    for j in range(3):
        hits = (sw_col == iota((SWP, 128), 1) + 128 * j).astype(f32)
        flags.append(jnp.sum(hits, 0, keepdims=True))
        own_h = own_h + jnp.sum(hits * own_r[j : j + 1], 1, keepdims=True)
        node_h = node_h + jnp.sum(hits * node_r[j : j + 1], 1, keepdims=True)
    own_h = jnp.where(sw_row < SW, jnp.broadcast_to(own_h, (SWP, 128)), -1.0)
    node_h = jnp.broadcast_to(node_h, (SWP, 128))

    parts = channels(PB, SWP, 3)
    lo_s = iota((SWP, 128), 1) < 64
    hs1[...] = jnp.concatenate(
        [parts[0], parts[1], jnp.where(lo_s, parts[2], node_h), own_h], 1
    ).astype(bf16)

    pl.semaphore_wait(bar, OWN - 1)
    hand1 = partner_copies(hs1, hr1, 0)
    for c in hand1:
        c.start()
    lax.fori_loop(EARLY * CHP // GROUP, NAT, scatter_group, 0)

    own_cols = []
    for j in range(3):
        lanes = slice(j * 128, j * 128 + 128)
        own_j = jnp.where(flags[j] > 0.0, -1.0, own_r[j : j + 1])
        own_b = jnp.broadcast_to(own_j, (128, 128))
        kr_ref[:, lanes] = own_b
        own_cols.append(own_b.T)
        node_c = jnp.broadcast_to(node_r[j : j + 1], (128, 128)).T
        parts = channels(j * 128, 128, 3)
        lo_b = iota((128, 128), 1) < 64
        pb_ref[lanes, :] = jnp.concatenate(
            [parts[0], parts[1], jnp.where(lo_b, parts[2], node_c)], 1
        ).astype(bf16)
    pb_ref[PB:EXT, :] = jnp.zeros((EXT - PB, 384), bf16)

    for c in hand1:
        c.wait()
    got = picked(hr1)
    pb_ref[PB : PB + SWP, :] = got[:, 0:384].astype(bf16)
    own_cols.append(jnp.concatenate([got[:, 384:512], jnp.full((96, 128), -1.0, f32)], 0))
    kr_ref[:, PB:EXT] = own_cols[3].T

    before = iota((128, 128), 1) < iota((128, 128), 0)
    for i in range(4):
        count = jnp.zeros((128, 128), f32)
        for j in range(i + 1):
            same = own_cols[i] == kr_ref[:, j * 128 : j * 128 + 128]
            if j == i:
                same = jnp.logical_and(same, before)
            count = count + jnp.where(same, 1.0, 0.0)
        rank = jnp.broadcast_to(jnp.sum(count, 1, keepdims=True), (128, 128))
        key = jnp.where(own_cols[i] >= 0.0, own_cols[i] * SLOTS + rank, -1.0)
        kc_ref[i * 128 : i * 128 + 128, :] = key
    for i in range(4):
        kr_ref[:, i * 128 : i * 128 + 128] = kc_ref[i * 128 : i * 128 + 128, :].T

    def send_rows(c, groups):
        rows = pl.ds(pl.multiple_of(c * 128, 128), 128)
        if groups == 3:
            r = iota((128, EXT), 0) + c * 128
            row_key = ((r // 8) * SLOTS + r % SLOTS).astype(f32)
            pick = jnp.where(row_key == kr_ref[...], 1.0, 0.0).astype(bf16)
            pick_ref[rows, :] = pick
        else:
            pick = pick_ref[rows, :]
        res = dot(pick, pb_ref[:, 0 : groups * 128])
        first_half = (iota((128, 128), 0) % 8) < SLOTS
        main = jnp.where(first_half, res[:, 0:128], res[:, 128:256])
        return main.reshape(16, 8, 128), res[:, 256:]

    def fill1(c):
        main, extra = send_rows(c, 3)
        owners = pl.ds(pl.multiple_of(c * 16, 16), 16)
        send1[owners] = jnp.concatenate([main, extra.reshape(16, 8, 128)], 1).astype(bf16)

    all_to_all(fill1, send1, recv1, 0)

    key_lane = iota((EXT, 128), 1)
    for c in range(8):
        lane_key = (((key_lane + c * 128) // 8) * SLOTS + key_lane % SLOTS).astype(f32)
        sd_ref[:, c * 128 : c * 128 + 128] = jnp.where(
            kc_ref[...] == lane_key, 1.0, 0.0
        ).astype(bf16)

    all_to_all_wait(send1, recv1, 0)

    half0 = (iota((128, 128), 0) % 8) < SLOTS
    node_lane = (iota((128, 128), 1) - (NBD - 1)).astype(f32)

    def grid_sum1(c):
        blocks = recv1[c * 16 : c * 16 + 16].astype(f32)
        main = blocks[:, 0:8].reshape(128, 128)
        extra = blocks[:, 8:16].reshape(128, 128)
        hit = jnp.where(
            jnp.logical_and(extra == node_lane, node_lane > 0.0), 1.0, 0.0
        )
        at_ref[c * 128 : c * 128 + 128, :] = hit.astype(bf16)
        hit_t = hit.T.astype(bf16)
        a_ref[:, c * 128 : c * 128 + 128] = hit_t
        rhs = jnp.concatenate(
            [
                jnp.where(half0, main, 0.0),
                jnp.where(half0, 0.0, main),
                jnp.where(half0, extra, 0.0),
            ],
            1,
        ).astype(bf16)
        return dot(hit_t, rhs)

    def grid_sum2(c):
        main = recv2[c * 16 : c * 16 + 16].astype(f32).reshape(128, 128)
        rhs = jnp.concatenate(
            [jnp.where(half0, main, 0.0), jnp.where(half0, 0.0, main)], 1
        ).astype(bf16)
        return dot(a_ref[:, c * 128 : c * 128 + 128], rhs)

    lane_n = iota((NBD, 128), 1)
    keep0 = (lane_n % 64) >= 8
    keep1 = jnp.logical_or(lane_n >= 64, lane_n >= 8)

    def grid_fields(total, msafe):
        vel = jnp.where(keep0, total[NBD:, 0:128] / msafe, 0.0)
        rest = jnp.where(keep1, total[NBD:, 128:256] / msafe, 0.0)
        return jnp.concatenate([vel, rest], 1).astype(bf16)

    def answer(fields, ph):
        rhs = jnp.concatenate([jnp.zeros((NBD, 256), bf16), fields], 0)

        def fill(c):
            rows = pl.ds(pl.multiple_of(c * 128, 128), 128)
            res = dot(at_ref[rows, :], rhs)
            main = jnp.where(half0, res[:, 0:128], res[:, 128:256])
            owners = pl.ds(pl.multiple_of(c * 16, 16), 16)
            ans_s[ph, owners] = main.reshape(16, 8, 128).astype(bf16)

        all_to_all(fill, ans_s.at[ph], ans_r.at[ph], 1 + 2 * ph)

    def put_fields(first, count, fields):
        flat = fbx_ref.reshape(EXT * 8, 128)
        a, b = fields[0:count, 0:128], fields[0:count, 128:256]
        for g, val in enumerate((a, b, pltpu.roll(a, 64, 1), pltpu.roll(b, 64, 1))):
            flat[pl.ds(first * 8 + g, count, stride=8), :] = val

    def spread(src, ph):
        parts = []
        handed = jnp.zeros((SWP, 256), f32)
        for c in range(4):
            main = src[c * 32 : c * 32 + 32].astype(f32).reshape(256, 128)
            first_half = (iota((256, 128), 0) % 8) < SLOTS
            rhs = jnp.concatenate(
                [jnp.where(first_half, main, 0.0), jnp.where(first_half, 0.0, main)], 1
            ).astype(bf16)
            handed = handed + dot(sd_ref[PB : PB + SWP, c * 256 : c * 256 + 256], rhs)
            parts.append(rhs)
        fs[ph] = handed.astype(bf16)
        copies = partner_copies(fs.at[ph], fr.at[ph], 1 + ph)
        for c in copies:
            c.start()
        total = jnp.zeros((PB, 256), f32)
        for c in range(4):
            total = total + dot(sd_ref[0:PB, c * 256 : c * 256 + 256], parts[c])
        put_fields(0, PB, total)
        return copies

    def spread_end(copies, ph):
        for c in copies:
            c.wait()
        got = picked(fr.at[ph])
        put_fields(PB, SWP, got)

    total = grid_sum1(0)
    for c in range(1, 8):
        total = total + grid_sum1(c)
    mass_n = total[NBD:, 256:384]
    msafe = jnp.maximum(jnp.where(lane_n < 64, mass_n, pltpu.roll(mass_n, 64, 1)), 0.25)
    ms_ref[...] = msafe
    answer(grid_fields(total, msafe), 0)
    all_to_all_wait(ans_s.at[0], ans_r.at[0], 1)

    copies = spread(ans_r.at[0], 0)
    lax.fori_loop(0, NAT // 2, middle_group, 0)
    spread_end(copies, 0)
    lax.fori_loop(NAT, ALLP // GROUP, middle_group, 0)
    hs2[...] = jnp.concatenate(channels(PB, SWP, 2), 1).astype(bf16)
    hand2 = partner_copies(hs2, hr2, 3)
    for c in hand2:
        c.start()
    lax.fori_loop(NAT // 2, NAT, middle_group, 0)
    for j in range(3):
        pb_ref[j * 128 : j * 128 + 128, 0:256] = jnp.concatenate(
            channels(j * 128, 128, 2), 1
        ).astype(bf16)
    for c in hand2:
        c.wait()
    pb_ref[PB : PB + SWP, 0:256] = picked(hr2).astype(bf16)

    def fill2(c):
        main, _ = send_rows(c, 2)
        send2[pl.ds(pl.multiple_of(c * 16, 16), 16)] = main.astype(bf16)

    all_to_all(fill2, send2, recv2, 2)
    all_to_all_wait(send2, recv2, 2)
    total = grid_sum2(0)
    for c in range(1, 8):
        total = total + grid_sum2(c)
    fields = grid_fields(total, ms_ref[...])
    field_ref[...] = fields
    answer(fields, 1)
    all_to_all_wait(ans_s.at[1], ans_r.at[1], 3)

    copies = spread(ans_r.at[1], 1)
    lax.fori_loop(0, NAT // 2, last_group, 0)
    spread_end(copies, 1)
    lax.fori_loop(NAT, ALLP // GROUP, last_extra, 0)
    hand3 = partner_copies(xs, xr, 4)
    for c in hand3:
        c.start()
    lax.fori_loop(NAT // 2, NAT, last_group, 0)
    for c in hand3:
        c.wait()
    xout_ref[...] = picked(xr)


def weld_call(weights, state, mass, stiff, targets, counts, bit, swap):
    vmem = pl.BlockSpec(memory_space=pltpu.VMEM)
    smem = pl.BlockSpec(memory_space=pltpu.SMEM)
    dma = pltpu.SemaphoreType.DMA
    return pl.pallas_call(
        weld_kernel,
        out_shape=(
            jax.ShapeDtypeStruct((10, PB * BS), f32),
            jax.ShapeDtypeStruct((NBD, 4 * BS), bf16),
            jax.ShapeDtypeStruct((16, XPAIRS * 128), f32),
        ),
        in_specs=[pl.BlockSpec(memory_space=pl.ANY), vmem, vmem, vmem, vmem, smem, smem, smem],
        out_specs=(vmem, vmem, vmem),
        scratch_shapes=[
            pltpu.VMEM((2 * ALLP, BS, 4 * BS), bf16),
            pltpu.VMEM((ALLP, 8, 128), f32),
            pltpu.VMEM((ALLP, 8, 128), f32),
            pltpu.VMEM((ALLP, 8, 128), f32),
            pltpu.VMEM((ALLP, 8, 128), f32),
            pltpu.VMEM((ALLP, 8, 128), f32),
            pltpu.VMEM((ALLP, 8, 128), f32),
            pltpu.VMEM((EXT * 8, 128), f32),
            pltpu.VMEM((EXT, 384), bf16),
            pltpu.VMEM((EXT, 8, 128), f32),
            pltpu.VMEM((EXT, 128), f32),
            pltpu.VMEM((128, EXT), f32),
            pltpu.VMEM((EXT, ROWS), bf16),
            pltpu.VMEM((ROWS, EXT), bf16),
            pltpu.VMEM((ROWS, 128), bf16),
            pltpu.VMEM((128, ROWS), bf16),
            pltpu.VMEM((NBD, 128), f32),
            pltpu.VMEM((OWN, 16, 128), bf16),
            pltpu.VMEM((OWN, 16, 128), bf16),
            pltpu.VMEM((OWN, 8, 128), bf16),
            pltpu.VMEM((OWN, 8, 128), bf16),
            pltpu.VMEM((2, OWN, 8, 128), bf16),
            pltpu.VMEM((2, OWN, 8, 128), bf16),
            pltpu.VMEM((SWP, 512), bf16),
            pltpu.VMEM((2, SWP, 512), bf16),
            pltpu.VMEM((SWP, 256), bf16),
            pltpu.VMEM((2, SWP, 256), bf16),
            pltpu.VMEM((2, SWP, 256), bf16),
            pltpu.VMEM((2, 2, SWP, 256), bf16),
            pltpu.VMEM((16, XPAIRS * 128), f32),
            pltpu.VMEM((2, 16, XPAIRS * 128), f32),
            dma((CHUNKS,)),
            dma((4,)),
            dma((4,)),
            dma((5, 2)),
            dma((5, 2)),
        ],
        compiler_params=pltpu.CompilerParams(
            collective_id=0, has_side_effects=True, vmem_limit_bytes=56 * 1024 * 1024
        ),
    )(weights, state, mass, stiff, targets, counts, bit, swap)


def place_kernel(own_hbm, got_hbm, fields_hbm, swap_ref, out_ref, fields_out, got_ref, sem):
    copies = [
        pltpu.make_async_copy(src, dst, sem.at[i])
        for i, (src, dst) in enumerate(
            ((own_hbm, out_ref), (got_hbm, got_ref), (fields_hbm, fields_out))
        )
    ]
    for c in copies:
        c.start()
    lane = iota((8, 128), 1)
    for c in copies:
        c.wait()
    for s in range(SW):
        blk_id = swap_ref[0, s]
        src = slice((s // 2) * 128, (s // 2) * 128 + 128)
        dst = pl.ds(pl.multiple_of((blk_id // 2) * 128, 128), 128)
        same = (s % 2) == (blk_id % 2)
        mine = (lane >= 64) == (blk_id % 2 == 1)
        top, low = got_ref[0:8, src], got_ref[8:16, src]
        top = jnp.where(same, top, pltpu.roll(top, 64, 1))
        low = jnp.where(same, low, pltpu.roll(low, 64, 1))
        out_ref[0:8, dst] = jnp.where(mine, top, out_ref[0:8, dst])
        out_ref[8:10, dst] = jnp.where(mine[0:2], low[0:2], out_ref[8:10, dst])


def place_call(own, got, fields, swap):
    vmem = pl.BlockSpec(memory_space=pltpu.VMEM)
    hbm = pl.BlockSpec(memory_space=pl.ANY)
    return pl.pallas_call(
        place_kernel,
        out_shape=(
            jax.ShapeDtypeStruct((10, PB * BS), f32),
            jax.ShapeDtypeStruct((NBD, 4 * BS), bf16),
        ),
        in_specs=[hbm, hbm, hbm, pl.BlockSpec(memory_space=pltpu.SMEM)],
        out_specs=(vmem, hbm),
        scratch_shapes=[
            pltpu.VMEM((16, XPAIRS * 128), f32),
            pltpu.SemaphoreType.DMA((3,)),
        ],
        compiler_params=pltpu.CompilerParams(vmem_limit_bytes=56 * 1024 * 1024),
    )(own, got, fields, swap)


def shards(weights, particle_state, mass, stiffness, targets, counts, partner_bit, swap_list):
    own, fields, got = weld_call(
        weights,
        particle_state,
        mass.reshape(1, PB * BS),
        stiffness.reshape(1, PB * BS),
        targets.reshape(3, 128),
        counts,
        partner_bit,
        swap_list,
    )
    return place_call(own, got, fields, swap_list)


def solution(mesh):
    both = ("weld", "trans")
    in_specs = (
        P(both, None, None),
        P(None, both),
        P(both),
        P(both),
        P(both),
        P(both),
        P(both),
        P(both, None),
    )
    out_specs = (P(None, both), P(both, None))
    return jax.shard_map(shards, mesh=mesh, in_specs=in_specs, out_specs=out_specs, check_vma=False)
```
